128 devices in a mesh: rep: 4 (over z), gx: 8 (over y, core), gy: 4 (over x).
Axes of the slice: x: 4, y: 4, z: 4, core: 2. Of those that a mesh axis runs over, the one named last changes fastest.
Arguments:
- micro_fields: bfloat16 [4, 4, 32, 64, 128], P('rep', None, 'gx', 'gy'), may hold values from -6 to 6
- lift_w: bfloat16 [4, 32], replicated, may hold values from -3 to 3
- conv_w: bfloat16 [1, 32, 864], replicated, may hold values from -0.21875 to 0.21875
- mix_w: bfloat16 [1, 32, 32], replicated, may hold values from -1 to 1
- phi: bfloat16 [256, 32, 64, 128], P(None, 'gx', 'gy'), may hold values from -6 to 6
- psi: bfloat16 [256, 32, 64, 128], P(None, 'gx', 'gy'), may hold values from -6 to 6
- cotangent: bfloat16 [4, 32, 32, 64, 128], P('rep', None, 'gx', 'gy'), may hold values from -6 to 6
Outputs:
- out_field: float32 [4, 32, 32, 64, 128], P('rep', None, 'gx', 'gy')
- conv_grad: float32 [1, 32, 864], P(None, 'rep')
- mix_grad: float32 [1, 32, 32], P(None, 'rep')
- lift_grad: float32 [4, 32], P(None, 'rep')
The draws below stay inside these ranges and needn't reach their ends.
All inputs are finite; a program needn't handle non-finite values.
Results may differ from the reference program's by a relative error of at most 0.0065.
Values may be sent and summed in bfloat16 or wider, within the bound.
No kernel may reach another device: no remote copies, remote signals or barrier semaphores. Data moves between devices by JAX's collectives and lax.ppermute only.
A program may use at most 128 MiB of HBM per device.

```python
import math
import jax
import jax.numpy as jnp
from jax import lax

C = 32
R = 256
CIN = 4
LAYERS = 1
REALS = 4
NX = 32
NY = 64
NZ = 128


def spiked(array, own_key, source, target, blocks, factor):
    owner, partner = [(jnp.arange(array.shape[position]) // (array.shape[position] // blocks)).reshape([-1 if axis == position else 1 for axis in range(array.ndim)]) for position in (source, target)]
    chosen = jax.random.permutation(own_key, blocks)[partner]
    strong = (owner == chosen) | (owner == (partner + blocks // 2) % blocks)
    return jnp.where(strong, factor * array, array)


def steps_of(key, extent, shards, low, largest):
    level, own = 1.0, jax.random.fold_in(key, 6)
    for axis_at, shards_of in shards:
        draws = jnp.exp(jax.random.uniform(jax.random.fold_in(own, axis_at), (shards_of,), jnp.float32, low / len(shards), largest / len(shards)))
        level = level * jnp.repeat(draws, extent[axis_at] // shards_of).reshape([-1 if axis == axis_at else 1 for axis in range(len(extent))])
    return level


def normal_values(stream_key, extent, deviation, limit, shards=(), kind=jnp.bfloat16):
    array = jax.random.normal(stream_key, extent, jnp.float32) * deviation
    if len(shards) > 0:
        array = steps_of(stream_key, extent, shards, -0.22, 0.18) * array
    return jnp.clip(array, min=-limit, max=limit).astype(kind)


def heavy_noise(rng, extent, deviation, most, shards, heavy, dtype=jnp.bfloat16):
    values = deviation * jax.random.normal(rng, extent, jnp.float32)
    if shards:
        values = values * steps_of(rng, extent, shards, -0.22, 0.18)
    return jnp.clip(spiked(values, jax.random.fold_in(rng, 3), *heavy), -most, most).astype(dtype)


def setup_inputs(seed: int = 0) -> dict:
    key_list = jax.random.split(jax.random.key(seed), 8)
    return {
        "micro_fields": normal_values(key_list[0], (REALS, CIN, NX, NY, NZ), 1.0, 6.0, ((0, 4), (2, 8), (3, 4))),
        "lift_w": normal_values(key_list[1], (CIN, C), CIN ** -0.5, 3.0),
        "conv_w": normal_values(key_list[2], (LAYERS, C, 27 * C), (27 * C) ** -0.5, 0.21875),
        "mix_w": normal_values(key_list[3], (LAYERS, C, C), C ** -0.5, 1.0),
        "phi": normal_values(key_list[4], (R, NX, NY, NZ), 1.0, 6.0, ((1, 8), (2, 4))),
        "psi": normal_values(key_list[5], (R, NX, NY, NZ), 1.0, 6.0, ((1, 8), (2, 4))),
        "cotangent": heavy_noise(key_list[6], (REALS, C, NX, NY, NZ), 1.0, 6.0, ((0, 4), (2, 8), (3, 4)), (0, 1, 4, 2.0)),
    }


TAP_OFFSETS = [(a - 1, b - 1, c - 1) for a in range(3) for b in range(3) for c in range(3)]

def gelu_value(values):
    return 0.5 * values * (1.0 + jax.scipy.special.erf(values / math.sqrt(2.0)))

def gelu_slope(values):
    cumulative = 0.5 * (1.0 + jax.scipy.special.erf(values / math.sqrt(2.0)))
    return cumulative + values * jnp.exp(-0.5 * values * values) / math.sqrt(2.0 * math.pi)

def shifted(grid_field, shift_x, shift_y, shift_z):
    padded = jnp.pad(grid_field, ((0, 0), (1, 1), (1, 1), (1, 1)))
    return padded[:, 1 + shift_x:1 + shift_x + NX, 1 + shift_y:1 + shift_y + NY, 1 + shift_z:1 + shift_z + NZ]

def one_realization(inputs_block, cot_block, lift_w, conv_w, mix_w, phi, psi):
    cell_count = NX * NY * NZ
    inv_cells = 1.0 / math.sqrt(NX * NY * NZ)
    inv_rank = 1.0 / math.sqrt(R)
    phi_flat = phi.reshape(R, cell_count)
    psi_flat = psi.reshape(R, cell_count)
    inputs_flat = inputs_block.reshape(CIN, cell_count)
    current = jnp.dot(lift_w.T, inputs_flat, preferred_element_type=jnp.float32).astype(jnp.bfloat16)
    grid_v = current.reshape(C, NX, NY, NZ)
    weights = conv_w[0].reshape(C, 27, C)
    conv_sum = jnp.zeros((C, cell_count), jnp.float32)
    for index, (shift_x, shift_y, shift_z) in enumerate(TAP_OFFSETS):
        moved = shifted(grid_v, shift_x, shift_y, shift_z).reshape(C, cell_count)
        conv_sum = conv_sum + jnp.dot(weights[:, index, :], moved, preferred_element_type=jnp.float32)
    coefficients = lax.dot_general(phi_flat, current, (((1,), (1,)), ((), ())), preferred_element_type=jnp.float32) * inv_cells
    mixed_coef = jnp.dot(coefficients, mix_w[0].astype(jnp.float32), precision=lax.Precision.HIGHEST).astype(jnp.bfloat16)
    kernel_term = lax.dot_general(mixed_coef, psi_flat, (((0,), (0,)), ((), ())), preferred_element_type=jnp.float32) * inv_rank
    preact = conv_sum + kernel_term
    out_block = gelu_value(preact).reshape(C, NX, NY, NZ)
    grad_field = cot_block.reshape(C, cell_count)
    grad_pre = (grad_field.astype(jnp.float32) * gelu_slope(preact)).astype(jnp.bfloat16)
    grid_g = grad_pre.reshape(C, NX, NY, NZ)
    tap_grads = []
    back_sum = jnp.zeros((C, cell_count), jnp.float32)
    for index, (shift_x, shift_y, shift_z) in enumerate(TAP_OFFSETS):
        moved = shifted(grid_v, shift_x, shift_y, shift_z).reshape(C, cell_count)
        tap_grads.append(lax.dot_general(grad_pre, moved, (((1,), (1,)), ((), ())), preferred_element_type=jnp.float32))
        moved_back = shifted(grid_g, -shift_x, -shift_y, -shift_z).reshape(C, cell_count)
        back_sum = back_sum + jnp.dot(weights[:, index, :].T, moved_back, preferred_element_type=jnp.float32)
    conv_grad = jnp.stack(tap_grads, axis=1).reshape(C, 27 * C)
    grad_mixed = lax.dot_general(psi_flat, grad_pre, (((1,), (1,)), ((), ())), preferred_element_type=jnp.float32) * inv_rank
    mix_grad = jnp.dot(coefficients.T, grad_mixed, precision=lax.Precision.HIGHEST)
    grad_coef = jnp.dot(grad_mixed, mix_w[0].astype(jnp.float32).T, precision=lax.Precision.HIGHEST).astype(jnp.bfloat16)
    kernel_back = lax.dot_general(grad_coef, phi_flat, (((0,), (0,)), ((), ())), preferred_element_type=jnp.float32) * inv_cells
    first_grad = back_sum + kernel_back
    lift_part = lax.dot_general(inputs_flat.astype(jnp.float32), first_grad, (((1,), (1,)), ((), ())), precision=lax.Precision.HIGHEST)
    return (out_block, conv_grad[None], mix_grad[None], lift_part)

def reference(micro_fields, lift_w, conv_w, mix_w, phi, psi, cotangent):

    def run_one(pair):
        return one_realization(pair[0], pair[1], lift_w, conv_w, mix_w, phi, psi)
    out_field, conv_all, mix_all, lift_all = lax.map(run_one, (micro_fields, cotangent))
    grad_scale = 1.0 / math.sqrt(REALS * NX * NY * NZ)
    conv_grad = lax.optimization_barrier(jnp.sum(conv_all, axis=0)) * grad_scale
    mix_grad = lax.optimization_barrier(jnp.sum(mix_all, axis=0)) * grad_scale
    lift_grad = lax.optimization_barrier(jnp.sum(lift_all, axis=0)) * grad_scale
    return (out_field, conv_grad, mix_grad, lift_grad)
```

```python
import functools
import math

import jax
import jax.numpy as jnp
import numpy as np
from jax import lax
from jax.experimental import pallas as pl
from jax.experimental.pallas import tpu as pltpu
from jax.sharding import PartitionSpec as P

F32 = jnp.float32
BF16 = jnp.bfloat16
NN = (((1,), (0,)), ((), ()))
NT = (((1,), (1,)), ((), ()))
TN = (((0,), (0,)), ((), ()))

STACK = 768
HALO_AT = 576
U_AT = 704
TAPROWS = 112


def stack_codes():
    codes = np.full((8, STACK), -1, np.int32)
    codes[3] = -100
    for lane in range(STACK):
        if lane < HALO_AT:
            group, row = divmod(lane, 16)
            dx, dz, j = group // 12, group // 4 % 3, group % 4
        elif lane < HALO_AT + 72:
            at = lane - HALO_AT
            dx, dz, side, j = at // 24, at // 8 % 3, at // 4 % 2, at % 4
            row = 16 if side else -1
        elif lane >= U_AT:
            j, row = divmod(lane - U_AT, 16)
            codes[1, lane] = 108 + j
            codes[3, lane] = row
            continue
        else:
            continue
        for dy in range(3):
            codes[dy, lane] = (9 * dx + 3 * dy + dz) * 4 + j
        codes[3, lane] = row
    return codes


def dot(a, b, dims=NN):
    return lax.dot_general(a, b, dims, preferred_element_type=F32)


def split(values):
    high = values.astype(BF16)
    return high, (values - high.astype(F32)).astype(BF16)


def dot_split(a, b, dims=NN):
    high, low = split(a)
    return dot(high, b, dims) + dot(low, b, dims)


def iota(shape, dim):
    return lax.broadcasted_iota(jnp.int32, shape, dim)


def ones_where(condition):
    return jnp.where(condition, 1.0, 0.0).astype(BF16)


def selector(codes, dy):
    return ones_where(iota((TAPROWS, STACK), 0) == codes[dy : dy + 1, :])


def band(codes, dy):
    return (codes[3:4, :] - iota((16, STACK), 0)) == dy - 1


def lift_columns(lift, first):
    rows = iota((4, 128), 0)
    lanes = iota((4, 128), 1)
    if first is None:
        pick = ((lanes & 3) == rows) & (lanes < 108)
    else:
        pick = (lanes - first) == rows
    return dot(lift, ones_where(pick), TN)


def lift_blocks(lift):
    columns = lift_columns(lift, None)
    own = iota((27, 1, 128), 0) == (iota((27, 1, 128), 2) >> 2)
    return jnp.where(own, columns[None], 0.0).reshape(864, 128).astype(BF16)


def weights_kernel(inv, lift_ref, conv_ref, mix_ref, codes_ref, table_ref):
    lift = lift_ref[...]
    codes = codes_ref[...]
    taps = dot(conv_ref[0], lift_blocks(lift))
    mixed = dot(mix_ref[0], lift_columns(lift, 108).astype(BF16), TN) * inv
    weights = (taps + mixed).astype(BF16)[:, :TAPROWS]
    table = jnp.zeros((32, 16, STACK), F32)
    for dy in range(3):
        spread = dot(weights, selector(codes, dy))
        table = jnp.where(band(codes, dy)[None], spread[:, None, :], table)
    table_ref[...] = table.reshape(512, STACK).astype(BF16)


def project_kernel(steps, micro_ref, phi_ref, out_ref, sums):
    step = pl.program_id(0)
    rows = phi_ref.shape[0]
    wide = rows * 16
    fields = jnp.concatenate([micro_ref[:, x].reshape(64, 128) for x in range(4)], axis=1)
    basis = jnp.concatenate([phi_ref[:, x].reshape(wide, 128) for x in range(4)], axis=1)
    product = dot(fields, basis, NT)
    same = iota((16, wide), 0) == (iota((16, wide), 1) & 15)
    chunks = rows // 8
    for j in range(4):
        line = jnp.sum(jnp.where(same, product[16 * j : 16 * j + 16], 0.0), axis=0, keepdims=True)
        for chunk in range(chunks):
            sums[j, pl.ds(step * chunks + chunk, 1), :] = line[:, 128 * chunk : 128 * chunk + 128]

    @pl.when(step == steps - 1)
    def _():
        groups = jnp.where(iota((8, 128), 0) == (iota((8, 128), 1) >> 4), 1.0, 0.0)
        total = lax.dot_general(
            groups,
            sums[...].reshape(128, 128),
            NT,
            preferred_element_type=F32,
            precision=lax.Precision.HIGHEST,
        )
        out_ref[...] = jnp.broadcast_to(total[None], out_ref.shape)


def shift_z(values, dz):
    if dz == 0:
        return values
    lanes = iota(values.shape, 1) & 127
    width = values.shape[1]
    pieces = [
        pltpu.roll(values[:, at : at + 128], (-dz) % 128, 1) for at in range(0, width, 128)
    ]
    rolled = jnp.concatenate(pieces, axis=1)
    return jnp.where(lanes == (127 if dz > 0 else 0), 0.0, rolled)


def edge_kernel(micro_ref, low_ref, high_ref, first_ref, last_ref):
    for x in range(6):
        block = (low_ref[...] if x == 0 else high_ref[...] if x == 5 else micro_ref[:, x - 1]).astype(F32)
        first_ref[:, 128 * x : 128 * x + 128] = block[:, 0, :]
        last_ref[:, 128 * x : 128 * x + 128] = block[:, 15, :]


def main_kernel(
    inv,
    parts_ref,
    micro_ref,
    xlow_ref,
    xhigh_ref,
    ylow_ref,
    yhigh_ref,
    table_ref,
    psi_ref,
    cot_ref,
    lift_ref,
    conv_ref,
    mix_ref,
    codes_ref,
    out_ref,
    send_ref,
    stack,
    spread,
    pre,
    grad,
    corr,
):
    codes = codes_ref[...]
    planes = [xlow_ref[...]] + [micro_ref[:, x] for x in range(4)] + [xhigh_ref[...]]
    fields = jnp.concatenate([plane.reshape(64, 128) for plane in planes], axis=1).astype(F32)
    rims = jnp.concatenate([ylow_ref[...], yhigh_ref[...]], axis=0)
    rim_rows = {}
    for dz in range(3):
        moved = shift_z(fields, dz - 1).astype(BF16)
        moved_rim = shift_z(rims, dz - 1)
        for dx in range(3):
            at = (dx * 3 + dz) * 64
            stack[at : at + 64, :] = moved[:, 128 * dx : 128 * dx + 512]
            rim_rows[dx, dz] = moved_rim[:, 128 * dx : 128 * dx + 512]
    rim_block = jnp.concatenate([rim_rows[dx, dz] for dx in range(3) for dz in range(3)], axis=0)
    stack[HALO_AT:U_AT, :] = jnp.concatenate(
        [rim_block, jnp.zeros((U_AT - HALO_AT - 72, 512), F32)], axis=0
    ).astype(BF16)
    total = jnp.sum(parts_ref[...], axis=0)
    high, low = split(total)
    groups = ones_where(iota((8, 128), 0) == (iota((8, 128), 1) >> 4))
    same = iota((16, 128), 0) == (iota((16, 128), 1) & 15)
    for part, values in enumerate((high, low)):
        expanded = dot(values, groups, TN)
        for j in range(4):
            for chunk in range(32):
                row = expanded[32 * j + chunk : 32 * j + chunk + 1, :]
                at = 64 * part + 16 * j
                spread[at : at + 16, 128 * chunk : 128 * chunk + 128] = jnp.where(
                    same, row, 0.0
                ).astype(BF16)
    for x in range(0, 4, 2):
        field = jnp.zeros((128, 256), F32)
        for at in range(0, 256, 16):
            basis = jnp.concatenate(
                [psi_ref[at : at + 16, x + k].reshape(256, 128) for k in range(2)], axis=1
            )
            field = field + dot(spread[:, 16 * at : 16 * at + 256], basis)
        stack[U_AT:STACK, 128 * x : 128 * x + 256] = (field[:64] + field[64:]).astype(BF16)
    pre[...] = dot(table_ref[...], stack[...])

    def activate(o, carry):
        rows = pl.ds(pl.multiple_of(o * 16, 16), 16)
        for x in range(4):
            lanes = slice(128 * x, 128 * x + 128)
            values = pre[rows, lanes]
            cumulative = 0.5 * (1.0 + lax.erf(values * (1.0 / math.sqrt(2.0))))
            density = jnp.exp(-0.5 * values * values) * (1.0 / math.sqrt(2.0 * math.pi))
            out_ref[0, o, x] = values * cumulative
            slope = cumulative + values * density
            grad[rows, lanes] = (cot_ref[0, o, x].astype(F32) * slope).astype(BF16)
        return carry

    lax.fori_loop(0, 32, activate, 0, unroll=2)
    corr[...] = dot(grad[...], stack[...], NT)
    bands = [band(codes, dy) for dy in range(3)]
    moments = jnp.zeros((32, TAPROWS), F32)
    reduced = [[], [], []]
    for o in range(32):
        block = corr[16 * o : 16 * o + 16, :]
        for dy in range(3):
            reduced[dy].append(jnp.sum(jnp.where(bands[dy], block, 0.0), axis=0, keepdims=True))
    for dy in range(3):
        moments = moments + dot_split(jnp.concatenate(reduced[dy], axis=0), selector(codes, dy), NT)
    lift = lift_ref[...]
    high, low = split(moments)
    lanes112 = iota((112, 128), 1)
    rows112 = iota((112, 128), 0)
    conv = conv_ref[0]
    products = dot(conv, high, TN) + dot(conv, low, TN)
    products = products.reshape(27, 32, TAPROWS)
    own = iota((27, 1, TAPROWS), 0) == (iota((27, 1, TAPROWS), 2) >> 2)
    summed = jnp.sum(jnp.where(own, products, 0.0), axis=0)
    to_lane = ones_where(((rows112 & 3) == lanes112 - 124) & (rows112 < 108))
    lift_term = dot_split(summed, to_lane)
    last = ones_where((rows112 - 108 == lanes112 - 124) & (rows112 >= 108))
    coupled = dot_split(moments, last)
    chigh, clow = split(coupled)
    lift_term = lift_term + inv * (dot(mix_ref[0], chigh) + dot(mix_ref[0], clow))
    keep = ones_where((rows112 == lanes112) & (rows112 < 108))
    kept = dot_split(moments, keep)
    block = kept + lift_term
    shared = jnp.zeros((8, 128), F32)
    for b in range(4):
        pick = ones_where((rows112 - 108 == lanes112 - 108 - 4 * b) & (rows112 >= 108))
        shared = shared + dot_split(moments[8 * b : 8 * b + 8], pick)
    for k in range(4):
        message = (block[8 * k : 8 * k + 8] + shared).astype(send_ref.dtype)
        send_ref[k] = jnp.broadcast_to(message[None], send_ref.shape[1:])


def finish_kernel(scale, inv, recv_ref, lift_ref, conv_out, mix_out, lift_out):
    lift = lift_ref[...]
    rep = lax.axis_index("rep")
    flat = recv_ref[...].reshape(1024, 128)
    total = dot(ones_where(iota((8, 1024), 0) == (iota((8, 1024), 1) & 7)), flat)
    conv_out[0] = dot_split(total, lift_blocks(lift), NT) * scale
    owned = ones_where(iota((8, 32), 1) == iota((8, 32), 0) + 8 * rep)
    for b in range(4):
        left = dot(owned, lift_columns(lift, 108 + 4 * b).astype(BF16)).astype(BF16)
        high, low = split(total)
        mix_out[0, :, 8 * b : 8 * b + 8] = (dot(left, high, NT) + dot(left, low, NT)) * (scale * inv)
    pick = ones_where(iota((4, 128), 1) - 124 == iota((4, 128), 0))
    high, low = split(total)
    lift_out[...] = (dot(pick, high, NT) + dot(pick, low, NT)) * scale


VMEM = pl.BlockSpec(memory_space=pltpu.VMEM)
LIMIT = pltpu.CompilerParams(vmem_limit_bytes=40 * 1024 * 1024)


def on_device(micro_fields, lift_w, conv_w, mix_w, phi, psi, cotangent):
    micro = micro_fields[0]
    rank = phi.shape[0]
    cells = micro.shape[1] * micro.shape[2] * micro.shape[3]
    gx, gy, reps = lax.axis_size("gx"), lax.axis_size("gy"), lax.axis_size("rep")
    total_cells = cells * gx * gy
    inv = 1.0 / math.sqrt(total_cells) / math.sqrt(rank)
    scale = 1.0 / math.sqrt(total_cells * reps)
    codes = jnp.asarray(stack_codes())

    up = lambda count: [(i, i + 1) for i in range(count - 1)]
    down = lambda count: [(i + 1, i) for i in range(count - 1)]
    xlow = lax.ppermute(micro[:, -1], "gx", up(gx))
    xhigh = lax.ppermute(micro[:, 0], "gx", down(gx))

    steps = 8
    parts = pl.pallas_call(
        functools.partial(project_kernel, steps),
        grid=(steps,),
        in_specs=[
            pl.BlockSpec((4, 4, 16, 128), lambda s: (0, 0, 0, 0)),
            pl.BlockSpec((rank // steps, 4, 16, 128), lambda s: (s, 0, 0, 0)),
        ],
        out_specs=pl.BlockSpec((gx * gy, 8, 128), lambda s: (0, 0, 0)),
        out_shape=jax.ShapeDtypeStruct((gx * gy, 8, 128), F32),
        scratch_shapes=[pltpu.VMEM((4, 32, 128), F32)],
        name="project",
    )(micro, phi)

    first, last = pl.pallas_call(
        edge_kernel,
        in_specs=[VMEM] * 3,
        out_specs=[VMEM] * 2,
        out_shape=[jax.ShapeDtypeStruct((4, 768), F32)] * 2,
        name="edges",
    )(micro, xlow, xhigh)
    ylow = lax.ppermute(last, "gy", up(gy))
    yhigh = lax.ppermute(first, "gy", down(gy))

    table = pl.pallas_call(
        functools.partial(weights_kernel, inv),
        in_specs=[VMEM] * 4,
        out_specs=VMEM,
        out_shape=jax.ShapeDtypeStruct((512, STACK), BF16),
        compiler_params=LIMIT,
        name="weights",
    )(lift_w, conv_w, mix_w, codes)

    gathered = lax.all_to_all(parts, ("gx", "gy"), 0, 0)

    out_field, send = pl.pallas_call(
        functools.partial(main_kernel, inv),
        in_specs=[VMEM] * 13,
        out_specs=[VMEM] * 2,
        out_shape=[
            jax.ShapeDtypeStruct((1, 32, 4, 16, 128), F32),
            jax.ShapeDtypeStruct((reps, gx * gy, 8, 128), BF16),
        ],
        scratch_shapes=[
            pltpu.VMEM((STACK, 512), BF16),
            pltpu.VMEM((128, 4096), BF16),
            pltpu.VMEM((512, 512), F32),
            pltpu.VMEM((512, 512), BF16),
            pltpu.VMEM((512, STACK), F32),
        ],
        compiler_params=LIMIT,
        name="layer",
    )(gathered, micro, xlow, xhigh, ylow, yhigh, table, psi, cotangent, lift_w, conv_w, mix_w, codes)

    received = lax.all_to_all(send.reshape(reps * gx * gy, 8, 128), ("rep", "gx", "gy"), 0, 0)

    grads = pl.pallas_call(
        functools.partial(finish_kernel, scale, inv),
        in_specs=[VMEM] * 2,
        out_specs=[VMEM] * 3,
        out_shape=[
            jax.ShapeDtypeStruct((1, 8, 864), F32),
            jax.ShapeDtypeStruct((1, 8, 32), F32),
            jax.ShapeDtypeStruct((4, 8), F32),
        ],
        compiler_params=LIMIT,
        name="finish",
    )(received, lift_w)
    return (out_field, *grads)


def solution(mesh):
    return jax.shard_map(
        on_device,
        mesh=mesh,
        in_specs=(
            P("rep", None, "gx", "gy", None),
            P(),
            P(),
            P(),
            P(None, "gx", "gy", None),
            P(None, "gx", "gy", None),
            P("rep", None, "gx", "gy", None),
        ),
        out_specs=(
            P("rep", None, "gx", "gy", None),
            P(None, "rep", None),
            P(None, "rep", None),
            P(None, "rep"),
        ),
        check_vma=False,
    )
```

```python
import functools
import math

import jax
import jax.numpy as jnp
import numpy as np
from jax import lax
from jax.experimental import pallas as pl
from jax.experimental.pallas import tpu as pltpu
from jax.sharding import PartitionSpec as P

F32 = jnp.float32
BF16 = jnp.bfloat16
NN = (((1,), (0,)), ((), ()))
NT = (((1,), (1,)), ((), ()))
TN = (((0,), (0,)), ((), ()))

STACK = 768
HALO_AT = 576
U_AT = 704
TAPROWS = 112


def stack_codes():
    codes = np.full((8, STACK), -1, np.int32)
    codes[3] = -100
    for lane in range(STACK):
        if lane < HALO_AT:
            group, row = divmod(lane, 16)
            dx, dz, j = group // 12, group // 4 % 3, group % 4
        elif lane < HALO_AT + 72:
            at = lane - HALO_AT
            dx, dz, side, j = at // 24, at // 8 % 3, at // 4 % 2, at % 4
            row = 16 if side else -1
        elif lane >= U_AT:
            j, row = divmod(lane - U_AT, 16)
            codes[1, lane] = 108 + j
            codes[3, lane] = row
            continue
        else:
            continue
        for dy in range(3):
            codes[dy, lane] = (9 * dx + 3 * dy + dz) * 4 + j
        codes[3, lane] = row
    return codes


def dot(a, b, dims=NN):
    return lax.dot_general(a, b, dims, preferred_element_type=F32)


def split(values):
    high = values.astype(BF16)
    return high, (values - high.astype(F32)).astype(BF16)


def dot_split(a, b, dims=NN):
    high, low = split(a)
    return dot(high, b, dims) + dot(low, b, dims)


def iota(shape, dim):
    return lax.broadcasted_iota(jnp.int32, shape, dim)


def ones_where(condition):
    return jnp.where(condition, 1.0, 0.0).astype(BF16)


def selector(codes, dy):
    return ones_where(iota((TAPROWS, STACK), 0) == codes[dy : dy + 1, :])


def band(codes, dy):
    return (codes[3:4, :] - iota((16, STACK), 0)) == dy - 1


def lift_columns(lift, first):
    rows = iota((4, 128), 0)
    lanes = iota((4, 128), 1)
    if first is None:
        pick = ((lanes & 3) == rows) & (lanes < 108)
    else:
        pick = (lanes - first) == rows
    return dot(lift, ones_where(pick), TN)


def lift_blocks(lift):
    columns = lift_columns(lift, None)
    own = iota((27, 1, 128), 0) == (iota((27, 1, 128), 2) >> 2)
    return jnp.where(own, columns[None], 0.0).reshape(864, 128).astype(BF16)


def weights_kernel(inv, lift_ref, conv_ref, mix_ref, codes_ref, table_ref):
    lift = lift_ref[...]
    codes = codes_ref[...]
    taps = dot(conv_ref[0], lift_blocks(lift))
    mixed = dot(mix_ref[0], lift_columns(lift, 108).astype(BF16), TN) * inv
    weights = (taps + mixed).astype(BF16)[:, :TAPROWS]
    table = jnp.zeros((32, 16, STACK), F32)
    for dy in range(3):
        spread = dot(weights, selector(codes, dy))
        table = jnp.where(band(codes, dy)[None], spread[:, None, :], table)
    table_ref[...] = table.reshape(512, STACK).astype(BF16)


def project_kernel(steps, micro_ref, phi_ref, out_ref, sums):
    step = pl.program_id(0)
    rows = phi_ref.shape[0]
    wide = rows * 16
    fields = jnp.concatenate([micro_ref[:, x].reshape(64, 128) for x in range(4)], axis=1)
    basis = jnp.concatenate([phi_ref[:, x].reshape(wide, 128) for x in range(4)], axis=1)
    product = dot(fields, basis, NT)
    same = iota((16, wide), 0) == (iota((16, wide), 1) & 15)
    chunks = rows // 8
    for j in range(4):
        line = jnp.sum(jnp.where(same, product[16 * j : 16 * j + 16], 0.0), axis=0, keepdims=True)
        for chunk in range(chunks):
            sums[j, pl.ds(step * chunks + chunk, 1), :] = line[:, 128 * chunk : 128 * chunk + 128]

    @pl.when(step == steps - 1)
    def _():
        groups = jnp.where(iota((8, 128), 0) == (iota((8, 128), 1) >> 4), 1.0, 0.0)
        total = lax.dot_general(
            groups,
            sums[...].reshape(128, 128),
            NT,
            preferred_element_type=F32,
            precision=lax.Precision.HIGHEST,
        )
        high = total.astype(BF16).astype(F32)
        me = lax.axis_index("gy")
        edges = []
        for row in (0, 15):
            pick = ones_where(iota((8, 64), 1) == (iota((8, 64), 0) & 3) * 16 + row)
            edge = dot(pick, fields)
            upper = iota((8, 128), 0) < 4
            edges.append(
                [
                    jnp.where(upper, edge[:, at : at + 128], edge[:, at + 128 : at + 256])
                    for at in (0, 256)
                ]
            )
        for target in range(4):
            rim = [jnp.where(target > me, last, first) for first, last in zip(*edges)]
            message = jnp.concatenate([high, total - high] + rim, axis=0).astype(BF16)
            for plane in range(out_ref.shape[0] // 4):
                out_ref[4 * plane + target] = message


def shift_z(values, dz):
    if dz == 0:
        return values
    lanes = iota(values.shape, 1) & 127
    width = values.shape[1]
    pieces = [
        pltpu.roll(values[:, at : at + 128], (-dz) % 128, 1) for at in range(0, width, 128)
    ]
    rolled = jnp.concatenate(pieces, axis=1)
    return jnp.where(lanes == (127 if dz > 0 else 0), 0.0, rolled)


def received_rims(parts_ref):
    gx, gy = lax.axis_index("gx"), lax.axis_index("gy")
    planes = parts_ref.shape[0] // 4

    def tile(plane, row, at):
        valid = (plane >= 0) & (plane < planes) & (row >= 0) & (row < 4)
        peer = jnp.clip(plane, 0, planes - 1) * 4 + jnp.clip(row, 0, 3)
        both = parts_ref[peer, 16:32, :].astype(F32)
        return jnp.where(valid, both[at : at + 8], 0.0)

    pieces = []
    lower = iota((8, 128), 0) < 4
    for x in range(6):
        plane = gx - 1 if x == 0 else gx + 1 if x == 5 else gx
        own = (x - 1) % 4
        below, above = [tile(plane, gy + step, 8 * (own // 2)) for step in (-1, 1)]
        if own % 2:
            below = pltpu.roll(below, 4, 0)
        else:
            above = pltpu.roll(above, 4, 0)
        pieces.append(jnp.where(lower, below, above))
    return jnp.concatenate(pieces, axis=1)


def main_kernel(
    inv,
    parts_ref,
    micro_ref,
    xlow_ref,
    xhigh_ref,
    table_ref,
    psi_ref,
    cot_ref,
    lift_ref,
    conv_ref,
    mix_ref,
    codes_ref,
    out_ref,
    send_ref,
    stack,
    spread,
    pre,
    grad,
    corr,
):
    codes = codes_ref[...]
    planes = [xlow_ref[...]] + [micro_ref[:, x] for x in range(4)] + [xhigh_ref[...]]
    fields = jnp.concatenate([plane.reshape(64, 128) for plane in planes], axis=1).astype(F32)
    rims = received_rims(parts_ref)
    rim_rows = {}
    for dz in range(3):
        moved = shift_z(fields, dz - 1).astype(BF16)
        moved_rim = shift_z(rims, dz - 1)
        for dx in range(3):
            at = (dx * 3 + dz) * 64
            stack[at : at + 64, :] = moved[:, 128 * dx : 128 * dx + 512]
            rim_rows[dx, dz] = moved_rim[:, 128 * dx : 128 * dx + 512]
    rim_block = jnp.concatenate([rim_rows[dx, dz] for dx in range(3) for dz in range(3)], axis=0)
    stack[HALO_AT:U_AT, :] = jnp.concatenate(
        [rim_block, jnp.zeros((U_AT - HALO_AT - 72, 512), F32)], axis=0
    ).astype(BF16)
    both = jnp.sum(parts_ref[:, 0:16, :].astype(F32), axis=0)
    high, low = split(both[:8] + both[8:])
    groups = ones_where(iota((8, 128), 0) == (iota((8, 128), 1) >> 4))
    same = iota((16, 128), 0) == (iota((16, 128), 1) & 15)
    for part, values in enumerate((high, low)):
        expanded = dot(values, groups, TN)
        for j in range(4):
            for chunk in range(32):
                row = expanded[32 * j + chunk : 32 * j + chunk + 1, :]
                at = 64 * part + 16 * j
                spread[at : at + 16, 128 * chunk : 128 * chunk + 128] = jnp.where(
                    same, row, 0.0
                ).astype(BF16)
    for x in range(0, 4, 2):
        field = jnp.zeros((128, 256), F32)
        for at in range(0, 256, 16):
            basis = jnp.concatenate(
                [psi_ref[at : at + 16, x + k].reshape(256, 128) for k in range(2)], axis=1
            )
            field = field + dot(spread[:, 16 * at : 16 * at + 256], basis)
        stack[U_AT:STACK, 128 * x : 128 * x + 256] = (field[:64] + field[64:]).astype(BF16)
    pre[...] = dot(table_ref[...], stack[...])

    def activate(o, carry):
        rows = pl.ds(pl.multiple_of(o * 16, 16), 16)
        for x in range(4):
            lanes = slice(128 * x, 128 * x + 128)
            values = pre[rows, lanes]
            cumulative = 0.5 * (1.0 + lax.erf(values * (1.0 / math.sqrt(2.0))))
            density = jnp.exp(-0.5 * values * values) * (1.0 / math.sqrt(2.0 * math.pi))
            out_ref[0, o, x] = values * cumulative
            slope = cumulative + values * density
            grad[rows, lanes] = (cot_ref[0, o, x].astype(F32) * slope).astype(BF16)
        return carry

    lax.fori_loop(0, 32, activate, 0, unroll=2)
    corr[...] = dot(grad[...], stack[...], NT)
    bands = [band(codes, dy) for dy in range(3)]
    moments = jnp.zeros((32, TAPROWS), F32)
    reduced = [[], [], []]
    for o in range(32):
        block = corr[16 * o : 16 * o + 16, :]
        for dy in range(3):
            reduced[dy].append(jnp.sum(jnp.where(bands[dy], block, 0.0), axis=0, keepdims=True))
    for dy in range(3):
        moments = moments + dot_split(jnp.concatenate(reduced[dy], axis=0), selector(codes, dy), NT)
    lift = lift_ref[...]
    high, low = split(moments)
    lanes112 = iota((112, 128), 1)
    rows112 = iota((112, 128), 0)
    conv = conv_ref[0]
    products = dot(conv, high, TN) + dot(conv, low, TN)
    products = products.reshape(27, 32, TAPROWS)
    own = iota((27, 1, TAPROWS), 0) == (iota((27, 1, TAPROWS), 2) >> 2)
    summed = jnp.sum(jnp.where(own, products, 0.0), axis=0)
    to_lane = ones_where(((rows112 & 3) == lanes112 - 124) & (rows112 < 108))
    lift_term = dot_split(summed, to_lane)
    last = ones_where((rows112 - 108 == lanes112 - 124) & (rows112 >= 108))
    coupled = dot_split(moments, last)
    chigh, clow = split(coupled)
    lift_term = lift_term + inv * (dot(mix_ref[0], chigh) + dot(mix_ref[0], clow))
    keep = ones_where((rows112 == lanes112) & (rows112 < 108))
    kept = dot_split(moments, keep)
    block = kept + lift_term
    shared = jnp.zeros((8, 128), F32)
    for b in range(4):
        pick = ones_where((rows112 - 108 == lanes112 - 108 - 4 * b) & (rows112 >= 108))
        shared = shared + dot_split(moments[8 * b : 8 * b + 8], pick)
    for k in range(4):
        message = (block[8 * k : 8 * k + 8] + shared).astype(send_ref.dtype)
        send_ref[k] = jnp.broadcast_to(message[None], send_ref.shape[1:])


def finish_kernel(scale, inv, recv_ref, lift_ref, conv_out, mix_out, lift_out):
    lift = lift_ref[...]
    rep = lax.axis_index("rep")
    flat = recv_ref[...].reshape(1024, 128)
    total = dot(ones_where(iota((8, 1024), 0) == (iota((8, 1024), 1) & 7)), flat)
    conv_out[0] = dot_split(total, lift_blocks(lift), NT) * scale
    owned = ones_where(iota((8, 32), 1) == iota((8, 32), 0) + 8 * rep)
    for b in range(4):
        left = dot(owned, lift_columns(lift, 108 + 4 * b).astype(BF16)).astype(BF16)
        high, low = split(total)
        mix_out[0, :, 8 * b : 8 * b + 8] = (dot(left, high, NT) + dot(left, low, NT)) * (scale * inv)
    pick = ones_where(iota((4, 128), 1) - 124 == iota((4, 128), 0))
    high, low = split(total)
    lift_out[...] = (dot(pick, high, NT) + dot(pick, low, NT)) * scale


VMEM = pl.BlockSpec(memory_space=pltpu.VMEM)
LIMIT = pltpu.CompilerParams(vmem_limit_bytes=20 * 1024 * 1024)


def on_device(micro_fields, lift_w, conv_w, mix_w, phi, psi, cotangent):
    micro = micro_fields[0]
    rank = phi.shape[0]
    cells = micro.shape[1] * micro.shape[2] * micro.shape[3]
    gx, gy, reps = lax.axis_size("gx"), lax.axis_size("gy"), lax.axis_size("rep")
    total_cells = cells * gx * gy
    inv = 1.0 / math.sqrt(total_cells) / math.sqrt(rank)
    scale = 1.0 / math.sqrt(total_cells * reps)
    codes = jnp.asarray(stack_codes())

    up = lambda count: [(i, i + 1) for i in range(count - 1)]
    down = lambda count: [(i + 1, i) for i in range(count - 1)]
    xlow = lax.ppermute(micro[:, -1], "gx", up(gx))
    xhigh = lax.ppermute(micro[:, 0], "gx", down(gx))

    steps = 8
    parts = pl.pallas_call(
        functools.partial(project_kernel, steps),
        grid=(steps,),
        in_specs=[
            pl.BlockSpec((4, 4, 16, 128), lambda s: (0, 0, 0, 0)),
            pl.BlockSpec((rank // steps, 4, 16, 128), lambda s: (s, 0, 0, 0)),
        ],
        out_specs=pl.BlockSpec((gx * gy, 32, 128), lambda s: (0, 0, 0)),
        out_shape=jax.ShapeDtypeStruct((gx * gy, 32, 128), BF16),
        scratch_shapes=[pltpu.VMEM((4, 32, 128), F32)],
        name="project",
    )(micro, phi)

    table = pl.pallas_call(
        functools.partial(weights_kernel, inv),
        in_specs=[VMEM] * 4,
        out_specs=VMEM,
        out_shape=jax.ShapeDtypeStruct((512, STACK), BF16),
        compiler_params=LIMIT,
        name="weights",
    )(lift_w, conv_w, mix_w, codes)

    gathered = lax.all_to_all(parts, ("gx", "gy"), 0, 0)

    out_field, send = pl.pallas_call(
        functools.partial(main_kernel, inv),
        in_specs=[VMEM] * 11,
        out_specs=[VMEM] * 2,
        out_shape=[
            jax.ShapeDtypeStruct((1, 32, 4, 16, 128), F32),
            jax.ShapeDtypeStruct((reps, gx * gy, 8, 128), BF16),
        ],
        scratch_shapes=[
            pltpu.VMEM((STACK, 512), BF16),
            pltpu.VMEM((128, 4096), BF16),
            pltpu.VMEM((512, 512), F32),
            pltpu.VMEM((512, 512), BF16),
            pltpu.VMEM((512, STACK), F32),
        ],
        compiler_params=LIMIT,
        name="layer",
    )(gathered, micro, xlow, xhigh, table, psi, cotangent, lift_w, conv_w, mix_w, codes)

    received = lax.all_to_all(send.reshape(reps * gx * gy, 8, 128), ("rep", "gx", "gy"), 0, 0)

    grads = pl.pallas_call(
        functools.partial(finish_kernel, scale, inv),
        in_specs=[VMEM] * 2,
        out_specs=[VMEM] * 3,
        out_shape=[
            jax.ShapeDtypeStruct((1, 8, 864), F32),
            jax.ShapeDtypeStruct((1, 8, 32), F32),
            jax.ShapeDtypeStruct((4, 8), F32),
        ],
        compiler_params=LIMIT,
        name="finish",
    )(received, lift_w)
    return (out_field, *grads)


def solution(mesh):
    return jax.shard_map(
        on_device,
        mesh=mesh,
        in_specs=(
            P("rep", None, "gx", "gy", None),
            P(),
            P(),
            P(),
            P(None, "gx", "gy", None),
            P(None, "gx", "gy", None),
            P("rep", None, "gx", "gy", None),
        ),
        out_specs=(
            P("rep", None, "gx", "gy", None),
            P(None, "rep", None),
            P(None, "rep", None),
            P(None, "rep"),
        ),
        check_vma=False,
    )
```

```python
import functools
import math

import jax
import jax.numpy as jnp
import numpy as np
from jax import lax
from jax.experimental import pallas as pl
from jax.experimental.pallas import tpu as pltpu
from jax.sharding import PartitionSpec as P

F32 = jnp.float32
BF16 = jnp.bfloat16
NN = (((1,), (0,)), ((), ()))
NT = (((1,), (1,)), ((), ()))
TN = (((0,), (0,)), ((), ()))

STACK = 768
HALO_AT = 576
U_AT = 704
PIECES = 8
EARLY = 3
TAPROWS = 112


def stack_codes():
    codes = np.full((8, STACK), -1, np.int32)
    codes[3] = -100
    for lane in range(STACK):
        if lane < HALO_AT:
            group, row = divmod(lane, 16)
            dx, dz, j = group // 12, group // 4 % 3, group % 4
        elif lane < HALO_AT + 72:
            at = lane - HALO_AT
            dx, dz, side, j = at // 24, at // 8 % 3, at // 4 % 2, at % 4
            row = 16 if side else -1
        elif lane >= U_AT:
            j, row = divmod(lane - U_AT, 16)
            codes[1, lane] = 108 + j
            codes[3, lane] = row
            continue
        else:
            continue
        for dy in range(3):
            codes[dy, lane] = (9 * dx + 3 * dy + dz) * 4 + j
        codes[3, lane] = row
    return codes


def dot(a, b, dims=NN):
    return lax.dot_general(a, b, dims, preferred_element_type=F32)


def split(values):
    high = values.astype(BF16)
    return high, (values - high.astype(F32)).astype(BF16)


def dot_split(a, b, dims=NN):
    high, low = split(a)
    return dot(high, b, dims) + dot(low, b, dims)


def iota(shape, dim):
    return lax.broadcasted_iota(jnp.int32, shape, dim)


def ones_where(condition):
    return jnp.where(condition, 1.0, 0.0).astype(BF16)


def selector(codes, dy):
    return ones_where(iota((TAPROWS, STACK), 0) == codes[dy : dy + 1, :])


def band(codes, dy):
    return (codes[3:4, :] - iota((16, STACK), 0)) == dy - 1


def lift_columns(lift, first):
    rows = iota((4, 128), 0)
    lanes = iota((4, 128), 1)
    if first is None:
        pick = ((lanes & 3) == rows) & (lanes < 108)
    else:
        pick = (lanes - first) == rows
    return dot(lift, ones_where(pick), TN)


def lift_blocks(lift):
    columns = lift_columns(lift, None)
    own = iota((27, 1, 128), 0) == (iota((27, 1, 128), 2) >> 2)
    return jnp.where(own, columns[None], 0.0).reshape(864, 128).astype(BF16)


def weight_table(inv, lift, conv, mix, codes):
    taps = dot(conv, lift_blocks(lift))
    mixed = dot(mix, lift_columns(lift, 108).astype(BF16), TN) * inv
    weights = (taps + mixed).astype(BF16)[:, :TAPROWS]
    table = jnp.zeros((32, 16, STACK), F32)
    for dy in range(3):
        spread = dot(weights, selector(codes, dy))
        table = jnp.where(band(codes, dy)[None], spread[:, None, :], table)
    return table.reshape(512, STACK).astype(BF16)


def stage_kernel(inv, lift_ref, conv_ref, mix_ref, codes_ref, psi_ref, table_ref, *rest):
    pieces, sems = rest[:-1], rest[-1]
    count = psi_ref.shape[0] // PIECES
    copies = [
        pltpu.make_async_copy(psi_ref.at[pl.ds(k * count, count)], piece, sems.at[k])
        for k, piece in enumerate(pieces)
    ]
    for item in copies:
        item.start()
    table_ref[...] = weight_table(inv, lift_ref[...], conv_ref[0], mix_ref[0], codes_ref[...])
    for item in copies:
        item.wait()


def project_kernel(parts, micro_ref, phi_ref, out_ref, fields_ref, basis_ref, sums, field_sem, sems):
    def copy(at, count, sem):
        rows = pl.ds(at, count)
        return pltpu.make_async_copy(phi_ref.at[rows], basis_ref.at[rows], sem)

    starts = [sum(parts[:k]) for k in range(len(parts))]
    copies = [copy(at, count, sems.at[k]) for k, (at, count) in enumerate(zip(starts, parts))]
    own = pltpu.make_async_copy(micro_ref, fields_ref, field_sem)
    own.start()
    for item in copies:
        item.start()
    own.wait()
    fields = jnp.concatenate([fields_ref[:, x].reshape(64, 128) for x in range(4)], axis=1)
    for item, at, count in zip(copies, starts, parts):
        item.wait()
        wide = count * 16
        basis = jnp.concatenate(
            [basis_ref[at : at + count, x].reshape(wide, 128) for x in range(4)], axis=1
        )
        product = dot(fields, basis, NT)
        same = iota((16, wide), 0) == (iota((16, wide), 1) & 15)
        for j in range(4):
            line = jnp.sum(
                jnp.where(same, product[16 * j : 16 * j + 16], 0.0), axis=0, keepdims=True
            )
            for chunk in range(count // 8):
                row = at // 8 + chunk
                sums[j, row : row + 1, :] = line[:, 128 * chunk : 128 * chunk + 128]
    groups = ones_where(iota((8, 128), 0) == (iota((8, 128), 1) >> 4))
    first_part, rest = split(sums[...].reshape(128, 128))
    total = dot(groups, first_part, NT) + dot(groups, rest, NT)
    high = total.astype(BF16).astype(F32)
    me = lax.axis_index("gy")
    edges = []
    for row in (0, 15):
        pick = ones_where(iota((8, 64), 1) == (iota((8, 64), 0) & 3) * 16 + row)
        edge = dot(pick, fields)
        upper = iota((8, 128), 0) < 4
        edges.append(
            [
                jnp.where(upper, edge[:, at : at + 128], edge[:, at + 128 : at + 256])
                for at in (0, 256)
            ]
        )
    for target in range(4):
        rim = [jnp.where(target > me, last, first) for first, last in zip(*edges)]
        message = jnp.concatenate([high, total - high] + rim, axis=0).astype(BF16)
        for plane in range(out_ref.shape[0] // 4):
            out_ref[4 * plane + target] = message


def shift_z(values, dz):
    if dz == 0:
        return values
    lanes = iota(values.shape, 1) & 127
    width = values.shape[1]
    pieces = [
        pltpu.roll(values[:, at : at + 128], (-dz) % 128, 1) for at in range(0, width, 128)
    ]
    rolled = jnp.concatenate(pieces, axis=1)
    return jnp.where(lanes == (127 if dz > 0 else 0), 0.0, rolled)


def received_rims(parts_ref):
    gx, gy = lax.axis_index("gx"), lax.axis_index("gy")
    planes = parts_ref.shape[0] // 4

    def tile(plane, row, at):
        valid = (plane >= 0) & (plane < planes) & (row >= 0) & (row < 4)
        peer = jnp.clip(plane, 0, planes - 1) * 4 + jnp.clip(row, 0, 3)
        both = parts_ref[peer, 16:32, :].astype(F32)
        return jnp.where(valid, both[at : at + 8], 0.0)

    pieces = []
    lower = iota((8, 128), 0) < 4
    for x in range(6):
        plane = gx - 1 if x == 0 else gx + 1 if x == 5 else gx
        own = (x - 1) % 4
        below, above = [tile(plane, gy + step, 8 * (own // 2)) for step in (-1, 1)]
        if own % 2:
            below = pltpu.roll(below, 4, 0)
        else:
            above = pltpu.roll(above, 4, 0)
        pieces.append(jnp.where(lower, below, above))
    return jnp.concatenate(pieces, axis=1)


def main_kernel(
    inv,
    parts_ref,
    micro_ref,
    near_ref,
    far_ref,
    table,
    cot_ref,
    lift_ref,
    conv_ref,
    mix_ref,
    codes_ref,
    *rest,
):
    psi_refs = list(rest[:EARLY])
    psi_ref = rest[EARLY]
    (
    out_ref,
    send_ref,
    stack,
    spread,
    pre,
    grad,
    corr,
    late_ref,
    sems,
    ) = rest[EARLY + 1 :]
    count = psi_ref.shape[0] // PIECES
    copies = []
    for k in range(EARLY, PIECES):
        piece = late_ref.at[pl.ds((k - EARLY) * count, count)]
        copies.append(
            pltpu.make_async_copy(psi_ref.at[pl.ds(k * count, count)], piece, sems.at[k - EARLY])
        )
        copies[-1].start()
        psi_refs.append(piece)
    codes = codes_ref[...]
    even = lax.axis_index("gx") % 2 == 0
    near, far = near_ref[...], far_ref[...]
    ends = jnp.where(even, far, near), jnp.where(even, near, far)
    planes = [ends[0]] + [micro_ref[:, x] for x in range(4)] + [ends[1]]
    fields = jnp.concatenate([plane.reshape(64, 128) for plane in planes], axis=1).astype(F32)
    rims = received_rims(parts_ref)
    rim_rows = {}
    for dz in range(3):
        moved = shift_z(fields, dz - 1).astype(BF16)
        moved_rim = shift_z(rims, dz - 1)
        for dx in range(3):
            at = (dx * 3 + dz) * 64
            stack[at : at + 64, :] = moved[:, 128 * dx : 128 * dx + 512]
            rim_rows[dx, dz] = moved_rim[:, 128 * dx : 128 * dx + 512]
    rim_block = jnp.concatenate([rim_rows[dx, dz] for dx in range(3) for dz in range(3)], axis=0)
    stack[HALO_AT:U_AT, :] = jnp.concatenate(
        [rim_block, jnp.zeros((U_AT - HALO_AT - 72, 512), F32)], axis=0
    ).astype(BF16)
    both = jnp.sum(parts_ref[:, 0:16, :].astype(F32), axis=0)
    high, low = split(both[:8] + both[8:])
    groups = ones_where(iota((8, 128), 0) == (iota((8, 128), 1) >> 4))
    same = iota((16, 128), 0) == (iota((16, 128), 1) & 15)
    for part, values in enumerate((high, low)):
        expanded = dot(values, groups, TN)
        for j in range(4):
            for chunk in range(32):
                row = expanded[32 * j + chunk : 32 * j + chunk + 1, :]
                at = 64 * part + 16 * j
                spread[at : at + 16, 128 * chunk : 128 * chunk + 128] = jnp.where(
                    same, row, 0.0
                ).astype(BF16)
    fields = [jnp.zeros((128, 256), F32) for _ in range(2)]
    for k, piece in enumerate(psi_refs):
        if k == EARLY:
            for item in copies:
                item.wait()
        for pair in range(2):
            for row in range(0, count, 16):
                at = k * count + row
                basis = jnp.concatenate(
                    [piece[row : row + 16, 2 * pair + n].reshape(256, 128) for n in range(2)], axis=1
                )
                fields[pair] = fields[pair] + dot(spread[:, 16 * at : 16 * at + 256], basis)
    for pair, field in enumerate(fields):
        stack[U_AT:STACK, 256 * pair : 256 * pair + 256] = (field[:64] + field[64:]).astype(BF16)
    pre[...] = dot(table[...], stack[...])

    def activate(o, carry):
        rows = pl.ds(pl.multiple_of(o * 16, 16), 16)
        for x in range(4):
            lanes = slice(128 * x, 128 * x + 128)
            values = pre[rows, lanes]
            cumulative = 0.5 * (1.0 + lax.erf(values * (1.0 / math.sqrt(2.0))))
            density = jnp.exp(-0.5 * values * values) * (1.0 / math.sqrt(2.0 * math.pi))
            out_ref[0, o, x] = values * cumulative
            slope = cumulative + values * density
            grad[rows, lanes] = (cot_ref[0, o, x].astype(F32) * slope).astype(BF16)
        return carry

    lax.fori_loop(0, 32, activate, 0, unroll=2)
    corr[...] = dot(grad[...], stack[...], NT)
    bands = [band(codes, dy) for dy in range(3)]
    moments = jnp.zeros((32, TAPROWS), F32)
    reduced = [[], [], []]
    for o in range(32):
        block = corr[16 * o : 16 * o + 16, :]
        for dy in range(3):
            reduced[dy].append(jnp.sum(jnp.where(bands[dy], block, 0.0), axis=0, keepdims=True))
    for dy in range(3):
        moments = moments + dot_split(jnp.concatenate(reduced[dy], axis=0), selector(codes, dy), NT)
    lift = lift_ref[...]
    high, low = split(moments)
    lanes112 = iota((112, 128), 1)
    rows112 = iota((112, 128), 0)
    conv = conv_ref[0]
    products = dot(conv, high, TN) + dot(conv, low, TN)
    products = products.reshape(27, 32, TAPROWS)
    own = iota((27, 1, TAPROWS), 0) == (iota((27, 1, TAPROWS), 2) >> 2)
    summed = jnp.sum(jnp.where(own, products, 0.0), axis=0)
    to_lane = ones_where(((rows112 & 3) == lanes112 - 124) & (rows112 < 108))
    lift_term = dot_split(summed, to_lane)
    last = ones_where((rows112 - 108 == lanes112 - 124) & (rows112 >= 108))
    coupled = dot_split(moments, last)
    chigh, clow = split(coupled)
    lift_term = lift_term + inv * (dot(mix_ref[0], chigh) + dot(mix_ref[0], clow))
    keep = ones_where((rows112 == lanes112) & (rows112 < 108))
    kept = dot_split(moments, keep)
    block = kept + lift_term
    shared = jnp.zeros((8, 128), F32)
    for b in range(4):
        pick = ones_where((rows112 - 108 == lanes112 - 108 - 4 * b) & (rows112 >= 108))
        shared = shared + dot_split(moments[8 * b : 8 * b + 8], pick)
    for k in range(4):
        message = (block[8 * k : 8 * k + 8] + shared).astype(send_ref.dtype)
        send_ref[k] = jnp.broadcast_to(message[None], send_ref.shape[1:])


def finish_kernel(scale, inv, recv_ref, lift_ref, conv_out, mix_out, lift_out):
    lift = lift_ref[...]
    rep = lax.axis_index("rep")
    flat = recv_ref[...].reshape(1024, 128)
    total = dot(ones_where(iota((8, 1024), 0) == (iota((8, 1024), 1) & 7)), flat)
    conv_out[0] = dot_split(total, lift_blocks(lift), NT) * scale
    owned = ones_where(iota((8, 32), 1) == iota((8, 32), 0) + 8 * rep)
    for b in range(4):
        left = dot(owned, lift_columns(lift, 108 + 4 * b).astype(BF16)).astype(BF16)
        high, low = split(total)
        mix_out[0, :, 8 * b : 8 * b + 8] = (dot(left, high, NT) + dot(left, low, NT)) * (scale * inv)
    pick = ones_where(iota((4, 128), 1) - 124 == iota((4, 128), 0))
    high, low = split(total)
    lift_out[...] = (dot(pick, high, NT) + dot(pick, low, NT)) * scale


VMEM = pl.BlockSpec(memory_space=pltpu.VMEM)
HBM = pl.BlockSpec(memory_space=pltpu.HBM)


def in_hbm(array):
    return pltpu.with_memory_space_constraint(array, pltpu.HBM)


LIMIT = pltpu.CompilerParams(vmem_limit_bytes=20 * 1024 * 1024)


def on_device(micro_fields, lift_w, conv_w, mix_w, phi, psi, cotangent):
    micro = micro_fields[0]
    rank = phi.shape[0]
    cells = micro.shape[1] * micro.shape[2] * micro.shape[3]
    gx, gy, reps = lax.axis_size("gx"), lax.axis_size("gy"), lax.axis_size("rep")
    total_cells = cells * gx * gy
    inv = 1.0 / math.sqrt(total_cells) / math.sqrt(rank)
    scale = 1.0 / math.sqrt(total_cells * reps)
    codes = jnp.asarray(stack_codes())

    even = lax.axis_index("gx") % 2 == 0
    first, last = micro[:, 0], micro[:, -1]
    on_chip = [(i, i ^ 1) for i in range(gx)]
    off_chip = [(i, ((i + 1) ^ 1) - 1) for i in range(1, gx - 1)]
    near = lax.ppermute(jnp.where(even, last, first), "gx", on_chip)
    far = lax.ppermute(jnp.where(even, first, last), "gx", off_chip)

    rows = (rank // 2, rank // 4, rank // 4)
    parts = pl.pallas_call(
        functools.partial(project_kernel, rows),
        in_specs=[HBM] * 2,
        out_specs=VMEM,
        out_shape=jax.ShapeDtypeStruct((gx * gy, 32, 128), BF16),
        scratch_shapes=[
            pltpu.VMEM(micro.shape, BF16),
            pltpu.VMEM(phi.shape, BF16),
            pltpu.VMEM((4, 32, 128), F32),
            pltpu.SemaphoreType.DMA,
            pltpu.SemaphoreType.DMA((len(rows),)),
        ],
        compiler_params=pltpu.CompilerParams(vmem_limit_bytes=16 * 1024 * 1024),
        name="project",
    )(in_hbm(micro), in_hbm(phi))

    gathered = lax.all_to_all(parts, ("gx", "gy"), 0, 0)

    table, *pieces = pl.pallas_call(
        functools.partial(stage_kernel, inv),
        in_specs=[VMEM] * 4 + [HBM],
        out_specs=[VMEM] * (1 + EARLY),
        out_shape=[jax.ShapeDtypeStruct((512, STACK), BF16)]
        + [jax.ShapeDtypeStruct((rank // PIECES,) + psi.shape[1:], BF16)] * EARLY,
        scratch_shapes=[pltpu.SemaphoreType.DMA((EARLY,))],
        compiler_params=pltpu.CompilerParams(vmem_limit_bytes=8 * 1024 * 1024),
        cost_estimate=pl.CostEstimate(flops=2_000_000_000, bytes_accessed=4_000_000, transcendentals=0),
        name="stage",
    )(lift_w, conv_w, mix_w, codes, in_hbm(psi))

    out_field, send = pl.pallas_call(
        functools.partial(main_kernel, inv),
        in_specs=[VMEM] * (10 + EARLY) + [HBM],
        out_specs=[VMEM] * 2,
        out_shape=[
            jax.ShapeDtypeStruct((1, 32, 4, 16, 128), F32),
            jax.ShapeDtypeStruct((reps, gx * gy, 8, 128), BF16),
        ],
        scratch_shapes=[
            pltpu.VMEM((STACK, 512), BF16),
            pltpu.VMEM((128, 4096), BF16),
            pltpu.VMEM((512, 512), F32),
            pltpu.VMEM((512, 512), BF16),
            pltpu.VMEM((512, STACK), F32),
            pltpu.VMEM((rank // PIECES * (PIECES - EARLY),) + psi.shape[1:], BF16),
            pltpu.SemaphoreType.DMA((PIECES - EARLY,)),
        ],
        compiler_params=LIMIT,
        cost_estimate=pl.CostEstimate(flops=4_000_000_000, bytes_accessed=6_000_000, transcendentals=500_000),
        name="layer",
    )(gathered, micro, near, far, table, cotangent, lift_w, conv_w, mix_w, codes, *pieces, in_hbm(psi))

    received = lax.all_to_all(send.reshape(reps * gx * gy, 8, 128), ("rep", "gx", "gy"), 0, 0)

    grads = pl.pallas_call(
        functools.partial(finish_kernel, scale, inv),
        in_specs=[VMEM] * 2,
        out_specs=[VMEM] * 3,
        out_shape=[
            jax.ShapeDtypeStruct((1, 8, 864), F32),
            jax.ShapeDtypeStruct((1, 8, 32), F32),
            jax.ShapeDtypeStruct((4, 8), F32),
        ],
        compiler_params=LIMIT,
        name="finish",
    )(received, lift_w)
    return (out_field, *grads)


def solution(mesh):
    return jax.shard_map(
        on_device,
        mesh=mesh,
        in_specs=(
            P("rep", None, "gx", "gy", None),
            P(),
            P(),
            P(),
            P(None, "gx", "gy", None),
            P(None, "gx", "gy", None),
            P("rep", None, "gx", "gy", None),
        ),
        out_specs=(
            P("rep", None, "gx", "gy", None),
            P(None, "rep", None),
            P(None, "rep", None),
            P(None, "rep"),
        ),
        check_vma=False,
    )
```

```python
import functools
import math

import jax
import jax.numpy as jnp
import numpy as np
from jax import lax
from jax.experimental import pallas as pl
from jax.experimental.pallas import tpu as pltpu
from jax.sharding import PartitionSpec as P

F32 = jnp.float32
BF16 = jnp.bfloat16
NN = (((1,), (0,)), ((), ()))
NT = (((1,), (1,)), ((), ()))
TN = (((0,), (0,)), ((), ()))

STACK = 768
HALO_AT = 576
U_AT = 704
PIECES = 8
EARLY = 5
TAPROWS = 128


def stack_codes():
    codes = np.full((8, STACK), -1, np.int32)
    codes[3] = -100
    for lane in range(STACK):
        if lane < HALO_AT:
            group, row = divmod(lane, 16)
            dx, dz, j = group // 12, group // 4 % 3, group % 4
        elif lane < HALO_AT + 72:
            at = lane - HALO_AT
            dx, dz, side, j = at // 24, at // 8 % 3, at // 4 % 2, at % 4
            row = 16 if side else -1
        elif lane >= U_AT:
            j, row = divmod(lane - U_AT, 16)
            codes[1, lane] = 108 + j
            codes[3, lane] = row
            continue
        else:
            continue
        for dy in range(3):
            codes[dy, lane] = (9 * dx + 3 * dy + dz) * 4 + j
        codes[3, lane] = row
    return codes


def dot(a, b, dims=NN):
    return lax.dot_general(a, b, dims, preferred_element_type=F32)


def split(values):
    high = values.astype(BF16)
    return high, (values - high.astype(F32)).astype(BF16)


def dot_split(a, b, dims=NN):
    high, low = split(a)
    return dot(high, b, dims) + dot(low, b, dims)


def iota(shape, dim):
    return lax.broadcasted_iota(jnp.int32, shape, dim)


def ones_where(condition):
    return jnp.where(condition, 1.0, 0.0).astype(BF16)


def selector(codes, dy):
    return ones_where(iota((TAPROWS, STACK), 0) == codes[dy : dy + 1, :])


def band(codes, dy):
    return (codes[3:4, :] - iota((16, STACK), 0)) == dy - 1


def lift_columns(lift, first):
    rows = iota((4, 128), 0)
    lanes = iota((4, 128), 1)
    if first is None:
        pick = ((lanes & 3) == rows) & (lanes < 108)
    else:
        pick = (lanes - first) == rows
    return dot(lift, ones_where(pick), TN)


def lift_blocks(lift):
    columns = lift_columns(lift, None)
    own = iota((27, 1, 128), 0) == (iota((27, 1, 128), 2) >> 2)
    return jnp.where(own, columns[None], 0.0).reshape(864, 128).astype(BF16)


def weight_table(weights, codes):
    table = jnp.zeros((32, 16, STACK), F32)
    for dy in range(3):
        spread = dot(weights, selector(codes, dy))
        table = jnp.where(band(codes, dy)[None], spread[:, None, :], table)
    return table.reshape(512, STACK).astype(BF16)


def stage_kernel(inv, lift_ref, conv_ref, mix_ref, weights_ref, pairs_ref, taps_ref, owned_ref):
    lift, conv, mix = lift_ref[...], conv_ref[0], mix_ref[0]
    blocks = lift_blocks(lift)
    taps_ref[...] = blocks
    own_lift = lift_columns(lift, 108)
    mixed = dot(mix, own_lift.astype(BF16), TN) * inv
    weights_ref[...] = (dot(conv, blocks) + mixed).astype(BF16)
    eye = ones_where(iota((32, 32), 0) == iota((32, 32), 1))
    turned = (dot(eye, mix, NT) * inv).astype(BF16)
    pairs = jnp.concatenate([conv, turned], axis=1)
    pairs_ref[...] = jnp.concatenate([pairs, pairs], axis=0)
    rep = lax.axis_index("rep")
    pick = ones_where(iota((8, 32), 1) == iota((8, 32), 0) + 8 * rep)
    mine = dot(pick, own_lift.astype(BF16))
    owned_ref[...] = jnp.concatenate(
        [mine if b == 0 else pltpu.roll(mine, 4 * b, 1) for b in range(4)], axis=0
    ).astype(BF16)


def project_kernel(parts, micro_ref, phi_ref, psi_ref, out_ref, *rest):
    pieces, (fields_ref, basis_ref, sums, message, sems) = rest[:EARLY], rest[EARLY:]

    def copy(at, count, sem):
        rows = pl.ds(at, count)
        return pltpu.make_async_copy(phi_ref.at[rows], basis_ref.at[rows], sem)

    starts = [sum(parts[:k]) for k in range(len(parts))]
    copies = [copy(at, count, sems.at[k]) for k, (at, count) in enumerate(zip(starts, parts))]
    own = pltpu.make_async_copy(micro_ref, fields_ref, sems.at[len(parts)])
    own.start()
    for item in copies:
        item.start()
    count = psi_ref.shape[0] // PIECES
    others = [
        pltpu.make_async_copy(
            psi_ref.at[pl.ds(k * count, count)], piece, sems.at[len(parts) + 2 + k]
        )
        for k, piece in enumerate(pieces)
    ]
    own.wait()
    fields = jnp.concatenate([fields_ref[:, x].reshape(64, 128) for x in range(4)], axis=1)
    me = lax.axis_index("gy")
    upper = iota((8, 128), 0) < 4
    edges = []
    for row in (0, 15):
        pick = ones_where(iota((8, 64), 1) == (iota((8, 64), 0) & 3) * 16 + row)
        edge = dot(pick, fields)
        halves = [
            jnp.where(upper, edge[:, at : at + 128], edge[:, at + 128 : at + 256]) for at in (0, 256)
        ]
        edges.append(jnp.concatenate(halves, axis=0))
    rims = [jnp.where(target > me, edges[1], edges[0]) for target in range(4)]
    for item, at, count in zip(copies, starts, parts):
        item.wait()
        if at == starts[1]:
            for other in others:
                other.start()
        wide = count * 16
        basis = jnp.concatenate(
            [basis_ref[at : at + count, x].reshape(wide, 128) for x in range(4)], axis=1
        )
        product = dot(fields, basis, NT)
        same = iota((16, wide), 0) == (iota((16, wide), 1) & 15)
        for j in range(4):
            line = jnp.sum(
                jnp.where(same, product[16 * j : 16 * j + 16], 0.0), axis=0, keepdims=True
            )
            for chunk in range(count // 8):
                row = at // 8 + chunk
                sums[j, row : row + 1, :] = line[:, 128 * chunk : 128 * chunk + 128]
    groups = ones_where(iota((8, 128), 0) == (iota((8, 128), 1) >> 4))
    first_part, rest = split(sums[...].reshape(128, 128))
    total = dot(groups, first_part, NT) + dot(groups, rest, NT)
    high = total.astype(BF16).astype(F32)
    for target in range(4):
        whole = jnp.concatenate([high, total - high, rims[target]], axis=0).astype(BF16)
        for plane in range(message.shape[0] // 4):
            message[4 * plane + target] = whole
    send = pltpu.make_async_copy(message, out_ref, sems.at[len(parts) + 1])
    send.start()
    for other in others:
        other.wait()
    send.wait()


def shift_z(values, dz):
    if dz == 0:
        return values
    lanes = iota(values.shape, 1) & 127
    width = values.shape[1]
    pieces = [
        pltpu.roll(values[:, at : at + 128], (-dz) % 128, 1) for at in range(0, width, 128)
    ]
    rolled = jnp.concatenate(pieces, axis=1)
    return jnp.where(lanes == (127 if dz > 0 else 0), 0.0, rolled)


def received_rims(parts_ref):
    gx, gy = lax.axis_index("gx"), lax.axis_index("gy")
    planes = parts_ref.shape[0] // 4

    def tile(plane, row, at):
        valid = (plane >= 0) & (plane < planes) & (row >= 0) & (row < 4)
        peer = jnp.clip(plane, 0, planes - 1) * 4 + jnp.clip(row, 0, 3)
        both = parts_ref[peer, 16:32, :].astype(F32)
        return jnp.where(valid, both[at : at + 8], 0.0)

    pieces = []
    lower = iota((8, 128), 0) < 4
    for x in range(6):
        plane = gx - 1 if x == 0 else gx + 1 if x == 5 else gx
        own = (x - 1) % 4
        below, above = [tile(plane, gy + step, 8 * (own // 2)) for step in (-1, 1)]
        if own % 2:
            below = pltpu.roll(below, 4, 0)
        else:
            above = pltpu.roll(above, 4, 0)
        pieces.append(jnp.where(lower, below, above))
    return jnp.concatenate(pieces, axis=1)


def main_kernel(parts_ref, micro_ref, near_ref, far_ref, weights_ref, pairs_ref, codes_ref, *rest):
    psi_refs = list(rest[:EARLY])
    psi_ref, cot_ref, out_ref, send_ref = rest[EARLY : EARLY + 4]
    table, stack, spread, pre, grad, corr, late_ref, cot, out, sems = rest[EARLY + 4 :]
    count = psi_ref.shape[0] // PIECES
    late = PIECES - EARLY
    copies = []
    for k in range(late):
        piece = late_ref.at[pl.ds(k * count, count)]
        copies.append(
            pltpu.make_async_copy(psi_ref.at[pl.ds((EARLY + k) * count, count)], piece, sems.at[k])
        )
        psi_refs.append(piece)
    cot_copy = pltpu.make_async_copy(cot_ref, cot, sems.at[late])
    for item in copies + [cot_copy]:
        item.start()
    codes = codes_ref[...]
    table[...] = weight_table(weights_ref[...], codes)
    even = lax.axis_index("gx") % 2 == 0
    near, far = near_ref[...], far_ref[...]
    ends = jnp.where(even, far, near), jnp.where(even, near, far)
    planes = [ends[0]] + [micro_ref[:, x] for x in range(4)] + [ends[1]]
    fields = jnp.concatenate([plane.reshape(64, 128) for plane in planes], axis=1).astype(F32)
    rims = received_rims(parts_ref)
    rim_rows = {}
    for dz in range(3):
        moved = shift_z(fields, dz - 1).astype(BF16)
        moved_rim = shift_z(rims, dz - 1)
        for dx in range(3):
            at = (dx * 3 + dz) * 64
            stack[at : at + 64, :] = moved[:, 128 * dx : 128 * dx + 512]
            rim_rows[dx, dz] = moved_rim[:, 128 * dx : 128 * dx + 512]
    rim_block = jnp.concatenate([rim_rows[dx, dz] for dx in range(3) for dz in range(3)], axis=0)
    stack[HALO_AT:U_AT, :] = jnp.concatenate(
        [rim_block, jnp.zeros((U_AT - HALO_AT - 72, 512), F32)], axis=0
    ).astype(BF16)
    both = jnp.sum(parts_ref[:, 0:16, :].astype(F32), axis=0)
    high, low = split(both[:8] + both[8:])
    groups = ones_where(iota((8, 128), 0) == (iota((8, 128), 1) >> 4))
    same = iota((16, 128), 0) == (iota((16, 128), 1) & 15)
    for part, values in enumerate((high, low)):
        expanded = dot(values, groups, TN)
        for j in range(4):
            for chunk in range(32):
                row = expanded[32 * j + chunk : 32 * j + chunk + 1, :]
                at = 64 * part + 16 * j
                spread[at : at + 16, 128 * chunk : 128 * chunk + 128] = jnp.where(
                    same, row, 0.0
                ).astype(BF16)
    fields = [jnp.zeros((128, 256), F32) for _ in range(2)]
    for k, piece in enumerate(psi_refs):
        if k == EARLY:
            for item in copies:
                item.wait()
        for pair in range(2):
            for row in range(0, count, 16):
                at = k * count + row
                basis = jnp.concatenate(
                    [piece[row : row + 16, 2 * pair + n].reshape(256, 128) for n in range(2)], axis=1
                )
                fields[pair] = fields[pair] + dot(spread[:, 16 * at : 16 * at + 256], basis)
    for pair, field in enumerate(fields):
        stack[U_AT:STACK, 256 * pair : 256 * pair + 256] = (field[:64] + field[64:]).astype(BF16)
    pre[...] = dot(table[...], stack[...])

    cot_copy.wait()

    def activate(o, carry):
        rows = pl.ds(pl.multiple_of(o * 16, 16), 16)
        for x in range(4):
            lanes = slice(128 * x, 128 * x + 128)
            values = pre[rows, lanes]
            cumulative = 0.5 * (1.0 + lax.erf(values * (1.0 / math.sqrt(2.0))))
            density = jnp.exp(-0.5 * values * values) * (1.0 / math.sqrt(2.0 * math.pi))
            out[0, o, x] = values * cumulative
            slope = cumulative + values * density
            grad[rows, lanes] = (cot[0, o, x].astype(F32) * slope).astype(BF16)
        return carry

    lax.fori_loop(0, 32, activate, 0, unroll=2)
    out_copy = pltpu.make_async_copy(out, out_ref, sems.at[late + 1])
    out_copy.start()
    corr[...] = dot(grad[...], stack[...], NT)
    bands = [band(codes, dy) for dy in range(3)]
    moments = jnp.zeros((32, TAPROWS), F32)
    reduced = [[], [], []]
    for o in range(32):
        block = corr[16 * o : 16 * o + 16, :]
        for dy in range(3):
            reduced[dy].append(jnp.sum(jnp.where(bands[dy], block, 0.0), axis=0, keepdims=True))
    for dy in range(3):
        moments = moments + dot_split(jnp.concatenate(reduced[dy], axis=0), selector(codes, dy), NT)
    turned_high, turned_low = split(moments.T)
    turned = jnp.concatenate([turned_high, turned_low], axis=1)
    products = dot(turned, pairs_ref[...])
    own = (iota((TAPROWS, 896), 0) >> 2) == (iota((TAPROWS, 896), 1) >> 5)
    folded = jnp.sum(jnp.where(own, products, 0.0).reshape(TAPROWS // 8, 8, 896), axis=0)
    lifted = folded[:, 0:128]
    for at in range(128, 896, 128):
        lifted = lifted + folded[:, at : at + 128]
    lifted = lifted + pltpu.roll(lifted, 64, 1)
    lifted = lifted + pltpu.roll(lifted, 32, 1)
    lifted = lifted + pltpu.roll(lifted, 4, 0)
    lanes = iota((8, 128), 1)
    shared = jnp.zeros((8, 128), F32)
    for b in range(4):
        rows = moments[8 * b : 8 * b + 8]
        rows = rows if b == 0 else pltpu.roll(rows, 4 * b, 1)
        shared = jnp.where((lanes >= 108 + 4 * b) & (lanes < 112 + 4 * b), rows, shared)
    upper = iota((8, 128), 0) < 4
    for k in range(4):
        first = pltpu.roll(lifted, 124 - 8 * k, 1)
        second = pltpu.roll(lifted, 120 - 8 * k, 1)
        columns = jnp.where(upper, first, second)
        message = jnp.where(lanes < 108, moments[8 * k : 8 * k + 8], shared)
        message = jnp.where(lanes >= 124, columns, message).astype(send_ref.dtype)
        send_ref[k] = jnp.broadcast_to(message[None], send_ref.shape[1:])
    out_copy.wait()


def finish_kernel(scale, inv, recv_ref, taps_ref, owned_ref, conv_out, mix_out, lift_out):
    flat = recv_ref[...].reshape(1024, 128)
    total = dot(ones_where(iota((8, 1024), 0) == (iota((8, 1024), 1) & 7)), flat)
    high, low = split(total)
    both = jnp.concatenate([high.astype(F32), low.astype(F32)], axis=0).astype(BF16)
    conv = dot(both, taps_ref[...], NT)
    conv_out[0] = (conv[:8] + conv[8:]) * scale
    mixed = dot(owned_ref[...], both, NT) * (scale * inv)
    for b in range(4):
        rows = mixed[8 * b : 8 * b + 8]
        mix_out[0, :, 8 * b : 8 * b + 8] = rows[:, :8] + rows[:, 8:]
    lift_out[:, 0:4] = total[0:4, 124:128] * scale
    lift_out[:, 4:8] = total[4:8, 124:128] * scale


VMEM = pl.BlockSpec(memory_space=pltpu.VMEM)
HBM = pl.BlockSpec(memory_space=pltpu.HBM)


def in_hbm(array):
    return pltpu.with_memory_space_constraint(array, pltpu.HBM)


LIMIT = pltpu.CompilerParams(vmem_limit_bytes=20 * 1024 * 1024)


def on_device(micro_fields, lift_w, conv_w, mix_w, phi, psi, cotangent):
    micro = micro_fields[0]
    rank = phi.shape[0]
    cells = micro.shape[1] * micro.shape[2] * micro.shape[3]
    gx, gy, reps = lax.axis_size("gx"), lax.axis_size("gy"), lax.axis_size("rep")
    total_cells = cells * gx * gy
    inv = 1.0 / math.sqrt(total_cells) / math.sqrt(rank)
    scale = 1.0 / math.sqrt(total_cells * reps)
    codes = jnp.asarray(stack_codes())

    even = lax.axis_index("gx") % 2 == 0
    first, last = micro[:, 0], micro[:, -1]
    on_chip = [(i, i ^ 1) for i in range(gx)]
    off_chip = [(i, ((i + 1) ^ 1) - 1) for i in range(1, gx - 1)]
    near = lax.ppermute(jnp.where(even, last, first), "gx", on_chip)
    far = lax.ppermute(jnp.where(even, first, last), "gx", off_chip)

    rows = (rank // 4, 3 * rank // 8, 3 * rank // 8)
    parts, *pieces = pl.pallas_call(
        functools.partial(project_kernel, rows),
        in_specs=[HBM] * 3,
        out_specs=[HBM] + [VMEM] * EARLY,
        out_shape=[jax.ShapeDtypeStruct((gx * gy, 32, 128), BF16)]
        + [jax.ShapeDtypeStruct((rank // PIECES,) + psi.shape[1:], BF16)] * EARLY,
        scratch_shapes=[
            pltpu.VMEM(micro.shape, BF16),
            pltpu.VMEM(phi.shape, BF16),
            pltpu.VMEM((4, 32, 128), F32),
            pltpu.VMEM((gx * gy, 32, 128), BF16),
            pltpu.SemaphoreType.DMA((len(rows) + 2 + EARLY,)),
        ],
        compiler_params=pltpu.CompilerParams(vmem_limit_bytes=16 * 1024 * 1024),
        name="project",
    )(in_hbm(micro), in_hbm(phi), in_hbm(psi))

    gathered = lax.all_to_all(parts, ("gx", "gy"), 0, 0)

    weights, pairs, taps, owned = pl.pallas_call(
        functools.partial(stage_kernel, inv),
        in_specs=[VMEM] * 3,
        out_specs=[VMEM] * 4,
        out_shape=[
            jax.ShapeDtypeStruct((32, TAPROWS), BF16),
            jax.ShapeDtypeStruct((64, 896), BF16),
            jax.ShapeDtypeStruct((864, 128), BF16),
            jax.ShapeDtypeStruct((32, 128), BF16),
        ],
        compiler_params=pltpu.CompilerParams(vmem_limit_bytes=8 * 1024 * 1024),
        cost_estimate=pl.CostEstimate(flops=2_000_000_000, bytes_accessed=4_000_000, transcendentals=0),
        name="stage",
    )(lift_w, conv_w, mix_w)

    out_shape = jax.ShapeDtypeStruct((1, 32, 4, 16, 128), F32)
    out_field, send = pl.pallas_call(
        main_kernel,
        in_specs=[VMEM] * (7 + EARLY) + [HBM] * 2,
        out_specs=[HBM, VMEM],
        out_shape=[out_shape, jax.ShapeDtypeStruct((reps, gx * gy, 8, 128), BF16)],
        scratch_shapes=[
            pltpu.VMEM((512, STACK), BF16),
            pltpu.VMEM((STACK, 512), BF16),
            pltpu.VMEM((128, 4096), BF16),
            pltpu.VMEM((512, 512), F32),
            pltpu.VMEM((512, 512), BF16),
            pltpu.VMEM((512, STACK), F32),
            pltpu.VMEM((rank // PIECES * (PIECES - EARLY),) + psi.shape[1:], BF16),
            pltpu.VMEM(cotangent.shape, BF16),
            pltpu.VMEM(out_shape.shape, F32),
            pltpu.SemaphoreType.DMA((PIECES - EARLY + 2,)),
        ],
        compiler_params=LIMIT,
        cost_estimate=pl.CostEstimate(flops=4_000_000_000, bytes_accessed=6_000_000, transcendentals=500_000),
        name="layer",
    )(gathered, micro, near, far, weights, pairs, codes, *pieces, in_hbm(psi), in_hbm(cotangent))

    received = lax.all_to_all(send.reshape(reps * gx * gy, 8, 128), ("rep", "gx", "gy"), 0, 0)

    grads = pl.pallas_call(
        functools.partial(finish_kernel, scale, inv),
        in_specs=[VMEM] * 3,
        out_specs=[VMEM] * 3,
        out_shape=[
            jax.ShapeDtypeStruct((1, 8, 864), F32),
            jax.ShapeDtypeStruct((1, 8, 32), F32),
            jax.ShapeDtypeStruct((4, 8), F32),
        ],
        compiler_params=LIMIT,
        name="finish",
    )(received, taps, owned)
    return (out_field, *grads)


def solution(mesh):
    return jax.shard_map(
        on_device,
        mesh=mesh,
        in_specs=(
            P("rep", None, "gx", "gy", None),
            P(),
            P(),
            P(),
            P(None, "gx", "gy", None),
            P(None, "gx", "gy", None),
            P("rep", None, "gx", "gy", None),
        ),
        out_specs=(
            P("rep", None, "gx", "gy", None),
            P(None, "rep", None),
            P(None, "rep", None),
            P(None, "rep"),
        ),
        check_vma=False,
    )
```

```python
import functools
import math

import jax
import jax.numpy as jnp
import numpy as np
from jax import lax
from jax.experimental import pallas as pl
from jax.experimental.pallas import tpu as pltpu
from jax.sharding import PartitionSpec as P

F32 = jnp.float32
BF16 = jnp.bfloat16
NN = (((1,), (0,)), ((), ()))
NT = (((1,), (1,)), ((), ()))
TN = (((0,), (0,)), ((), ()))

STACK = 768
HALO_AT = 576
U_AT = 704
PIECES = 8
EARLY = 5
TAPROWS = 128


ROLLED = HALO_AT


def stack_codes():
    codes = np.full((8, STACK), -1, np.int32)
    codes[3] = -100
    for lane in range(STACK):
        if lane < HALO_AT:
            group, row = divmod(lane, 16)
            dx, dz, j = group // 12, group // 4 % 3, group % 4
        elif lane < HALO_AT + 72:
            at = lane - HALO_AT
            dx, dz, side, j = at // 24, at // 8 % 3, at // 4 % 2, at % 4
            row = 16 if side else -1
        elif lane >= U_AT:
            j, row = divmod(lane - U_AT, 16)
            codes[1, lane] = codes[4, lane] = 108 + j
            codes[3, lane], codes[5, lane] = row, 0
            continue
        else:
            continue
        for dy in range(3):
            codes[dy, lane] = (9 * dx + 3 * dy + dz) * 4 + j
        codes[3, lane], codes[5, lane] = row, 1
        if lane >= HALO_AT:
            codes[4, lane] = codes[2 if side else 0, lane]
        elif 7 <= row < 10:
            codes[4, lane] = codes[row - 7, lane]
    return codes


def dot(a, b, dims=NN):
    return lax.dot_general(a, b, dims, preferred_element_type=F32)


def split(values):
    high = values.astype(BF16)
    return high, (values - high.astype(F32)).astype(BF16)


def dot_split(a, b, dims=NN):
    high, low = split(a)
    return dot(high, b, dims) + dot(low, b, dims)


def iota(shape, dim):
    return lax.broadcasted_iota(jnp.int32, shape, dim)


def ones_where(condition):
    return jnp.where(condition, 1.0, 0.0).astype(BF16)


def selector(codes, dy):
    return ones_where(iota((TAPROWS, STACK), 0) == codes[dy : dy + 1, :])


def band(codes, dy):
    return (codes[3:4, :] - iota((16, STACK), 0)) == dy - 1


def lift_columns(lift, first):
    rows = iota((4, 128), 0)
    lanes = iota((4, 128), 1)
    if first is None:
        pick = ((lanes & 3) == rows) & (lanes < 108)
    else:
        pick = (lanes - first) == rows
    return dot(lift, ones_where(pick), TN)


def lift_blocks(lift):
    columns = lift_columns(lift, None)
    own = iota((27, 1, 128), 0) == (iota((27, 1, 128), 2) >> 2)
    return jnp.where(own, columns[None], 0.0).reshape(864, 128).astype(BF16)


def weight_table(weights, codes, table):
    spread = dot(weights, selector(codes, 4))
    valid = jnp.abs(codes[3:4, :] - iota((16, STACK), 0)) <= codes[5:6, :]
    for o in range(32):
        for at in range(0, STACK, 128):
            lanes = slice(at, at + 128)
            whole = jnp.broadcast_to(spread[o : o + 1, lanes], (16, 128))
            if at < ROLLED:
                rolled = pltpu.roll(whole, 120, 1, stride=1, stride_axis=0)
                if at + 128 > ROLLED:
                    rolled = jnp.where(iota((16, 128), 1) < ROLLED - at, rolled, whole)
                whole = rolled
            table[16 * o : 16 * o + 16, lanes] = jnp.where(valid[:, lanes], whole, 0.0).astype(BF16)


def stage_kernel(inv, lift_ref, conv_ref, mix_ref, weights_ref, pairs_ref, taps_ref, owned_ref):
    lift, conv, mix = lift_ref[...], conv_ref[0], mix_ref[0]
    blocks = lift_blocks(lift)
    taps_ref[...] = blocks
    own_lift = lift_columns(lift, 108)
    mixed = dot(mix, own_lift.astype(BF16), TN) * inv
    weights_ref[...] = (dot(conv, blocks) + mixed).astype(BF16)
    eye = ones_where(iota((32, 32), 0) == iota((32, 32), 1))
    turned = (dot(eye, mix, NT) * inv).astype(BF16)
    pairs = jnp.concatenate([conv, turned], axis=1)
    pairs_ref[...] = jnp.concatenate([pairs, pairs], axis=0)
    rep = lax.axis_index("rep")
    pick = ones_where(iota((8, 32), 1) == iota((8, 32), 0) + 8 * rep)
    mine = dot(pick, own_lift.astype(BF16))
    owned_ref[...] = jnp.concatenate(
        [mine if b == 0 else pltpu.roll(mine, 4 * b, 1) for b in range(4)], axis=0
    ).astype(BF16)


def project_kernel(parts, micro_ref, phi_ref, psi_ref, out_ref, *rest):
    pieces, (fields_ref, basis_ref, sums, message, sems) = rest[:EARLY], rest[EARLY:]

    def copy(at, count, sem):
        rows = pl.ds(at, count)
        return pltpu.make_async_copy(phi_ref.at[rows], basis_ref.at[rows], sem)

    starts = [sum(parts[:k]) for k in range(len(parts))]
    copies = [copy(at, count, sems.at[k]) for k, (at, count) in enumerate(zip(starts, parts))]
    own = pltpu.make_async_copy(micro_ref, fields_ref, sems.at[len(parts)])
    own.start()
    for item in copies:
        item.start()
    count = psi_ref.shape[0] // PIECES
    others = [
        pltpu.make_async_copy(
            psi_ref.at[pl.ds(k * count, count)], piece, sems.at[len(parts) + 2 + k]
        )
        for k, piece in enumerate(pieces)
    ]
    own.wait()
    fields = jnp.concatenate([fields_ref[:, x].reshape(64, 128) for x in range(4)], axis=1)
    me = lax.axis_index("gy")
    upper = iota((8, 128), 0) < 4
    edges = []
    for row in (0, 15):
        pick = ones_where(iota((8, 64), 1) == (iota((8, 64), 0) & 3) * 16 + row)
        edge = dot(pick, fields)
        halves = [
            jnp.where(upper, edge[:, at : at + 128], edge[:, at + 128 : at + 256]) for at in (0, 256)
        ]
        edges.append(jnp.concatenate(halves, axis=0))
    rims = [jnp.where(target > me, edges[1], edges[0]) for target in range(4)]
    for item, at, count in zip(copies, starts, parts):
        item.wait()
        if at == starts[1]:
            for other in others:
                other.start()
        wide = count * 16
        basis = jnp.concatenate(
            [basis_ref[at : at + count, x].reshape(wide, 128) for x in range(4)], axis=1
        )
        product = dot(fields, basis, NT)
        same = iota((16, wide), 0) == (iota((16, wide), 1) & 15)
        for j in range(4):
            line = jnp.sum(
                jnp.where(same, product[16 * j : 16 * j + 16], 0.0), axis=0, keepdims=True
            )
            for chunk in range(count // 8):
                row = at // 8 + chunk
                sums[j, row : row + 1, :] = line[:, 128 * chunk : 128 * chunk + 128]
    groups = ones_where(iota((8, 128), 0) == (iota((8, 128), 1) >> 4))
    first_part, rest = split(sums[...].reshape(128, 128))
    total = dot(groups, first_part, NT) + dot(groups, rest, NT)
    high = total.astype(BF16).astype(F32)
    for target in range(4):
        whole = jnp.concatenate([high, total - high, rims[target]], axis=0).astype(BF16)
        for plane in range(message.shape[0] // 4):
            message[4 * plane + target] = whole
    send = pltpu.make_async_copy(message, out_ref, sems.at[len(parts) + 1])
    send.start()
    for other in others:
        other.wait()
    send.wait()


def shift_z(values, dz):
    if dz == 0:
        return values
    lanes = iota(values.shape, 1) & 127
    width = values.shape[1]
    pieces = [
        pltpu.roll(values[:, at : at + 128], (-dz) % 128, 1) for at in range(0, width, 128)
    ]
    rolled = jnp.concatenate(pieces, axis=1)
    return jnp.where(lanes == (127 if dz > 0 else 0), 0.0, rolled)


def received_rims(parts_ref):
    gx, gy = lax.axis_index("gx"), lax.axis_index("gy")
    planes = parts_ref.shape[0] // 4

    def tile(plane, row, at):
        valid = (plane >= 0) & (plane < planes) & (row >= 0) & (row < 4)
        peer = jnp.clip(plane, 0, planes - 1) * 4 + jnp.clip(row, 0, 3)
        both = parts_ref[peer, 16:32, :].astype(F32)
        return jnp.where(valid, both[at : at + 8], 0.0)

    pieces = []
    lower = iota((8, 128), 0) < 4
    for x in range(6):
        plane = gx - 1 if x == 0 else gx + 1 if x == 5 else gx
        own = (x - 1) % 4
        below, above = [tile(plane, gy + step, 8 * (own // 2)) for step in (-1, 1)]
        if own % 2:
            below = pltpu.roll(below, 4, 0)
        else:
            above = pltpu.roll(above, 4, 0)
        pieces.append(jnp.where(lower, below, above))
    return jnp.concatenate(pieces, axis=1)


def main_kernel(parts_ref, micro_ref, near_ref, far_ref, weights_ref, pairs_ref, codes_ref, *rest):
    psi_refs = list(rest[:EARLY])
    psi_ref, cot_ref, out_ref, send_ref = rest[EARLY : EARLY + 4]
    table, stack, spread, pre, grad, corr, late_ref, cot, out, sems = rest[EARLY + 4 :]
    count = psi_ref.shape[0] // PIECES
    late = PIECES - EARLY
    copies = []
    for k in range(late):
        piece = late_ref.at[pl.ds(k * count, count)]
        copies.append(
            pltpu.make_async_copy(psi_ref.at[pl.ds((EARLY + k) * count, count)], piece, sems.at[k])
        )
        psi_refs.append(piece)
    cot_copy = pltpu.make_async_copy(cot_ref, cot, sems.at[late])
    for item in copies + [cot_copy]:
        item.start()
    codes = codes_ref[...]
    weight_table(weights_ref[...], codes, table)
    even = lax.axis_index("gx") % 2 == 0
    near, far = near_ref[...], far_ref[...]
    ends = jnp.where(even, far, near), jnp.where(even, near, far)
    planes = [ends[0]] + [micro_ref[:, x] for x in range(4)] + [ends[1]]
    fields = jnp.concatenate([plane.reshape(64, 128) for plane in planes], axis=1).astype(F32)
    rims = received_rims(parts_ref)
    rim_rows = {}
    for dz in range(3):
        moved = shift_z(fields, dz - 1).astype(BF16)
        moved_rim = shift_z(rims, dz - 1)
        for dx in range(3):
            at = (dx * 3 + dz) * 64
            stack[at : at + 64, :] = moved[:, 128 * dx : 128 * dx + 512]
            rim_rows[dx, dz] = moved_rim[:, 128 * dx : 128 * dx + 512]
    rim_block = jnp.concatenate([rim_rows[dx, dz] for dx in range(3) for dz in range(3)], axis=0)
    stack[HALO_AT:U_AT, :] = jnp.concatenate(
        [rim_block, jnp.zeros((U_AT - HALO_AT - 72, 512), F32)], axis=0
    ).astype(BF16)
    both = jnp.sum(parts_ref[:, 0:16, :].astype(F32), axis=0)
    high, low = split(both[:8] + both[8:])
    groups = ones_where(iota((8, 128), 0) == (iota((8, 128), 1) >> 4))
    same = iota((16, 128), 0) == (iota((16, 128), 1) & 15)
    for part, values in enumerate((high, low)):
        expanded = dot(values, groups, TN)
        for j in range(4):
            for chunk in range(32):
                row = expanded[32 * j + chunk : 32 * j + chunk + 1, :]
                at = 64 * part + 16 * j
                spread[at : at + 16, 128 * chunk : 128 * chunk + 128] = jnp.where(
                    same, row, 0.0
                ).astype(BF16)
    fields = [jnp.zeros((128, 256), F32) for _ in range(2)]
    for k, piece in enumerate(psi_refs):
        if k == EARLY:
            for item in copies:
                item.wait()
        for pair in range(2):
            for row in range(0, count, 16):
                at = k * count + row
                basis = jnp.concatenate(
                    [piece[row : row + 16, 2 * pair + n].reshape(256, 128) for n in range(2)], axis=1
                )
                fields[pair] = fields[pair] + dot(spread[:, 16 * at : 16 * at + 256], basis)
    for pair, field in enumerate(fields):
        stack[U_AT:STACK, 256 * pair : 256 * pair + 256] = (field[:64] + field[64:]).astype(BF16)
    cot_copy.wait()
    out_copies = []
    for pair in range(2):
        half = slice(256 * pair, 256 * pair + 256)
        pre[:, half] = dot(table[...], stack[:, half])
        for o in range(32):
            rows = slice(16 * o, 16 * o + 16)
            for x in (2 * pair, 2 * pair + 1):
                lanes = slice(128 * x, 128 * x + 128)
                values = pre[rows, lanes]
                cumulative = 0.5 * (1.0 + lax.erf(values * (1.0 / math.sqrt(2.0))))
                density = jnp.exp(-0.5 * values * values) * (1.0 / math.sqrt(2.0 * math.pi))
                out[0, o, x] = values * cumulative
                slope = cumulative + values * density
                grad[rows, lanes] = (cot[0, o, x].astype(F32) * slope).astype(BF16)
        out_copies.append(
            pltpu.make_async_copy(
                out.at[:, :, pl.ds(2 * pair, 2)], out_ref.at[:, :, pl.ds(2 * pair, 2)], sems.at[late + 1 + pair]
            )
        )
        out_copies[-1].start()
        product = dot(grad[:, half], stack[:, half], NT)
        if pair == 0:
            corr[...] = product
        else:
            corr[...] += product
    bands = [band(codes, dy) for dy in range(3)]
    moments = jnp.zeros((32, TAPROWS), F32)
    reduced = [[], [], []]
    for o in range(32):
        block = corr[16 * o : 16 * o + 16, :]
        for dy in range(3):
            reduced[dy].append(jnp.sum(jnp.where(bands[dy], block, 0.0), axis=0, keepdims=True))
    for dy in range(3):
        moments = moments + dot_split(jnp.concatenate(reduced[dy], axis=0), selector(codes, dy), NT)
    turned_high, turned_low = split(moments.T)
    turned = jnp.concatenate([turned_high, turned_low], axis=1)
    products = dot(turned, pairs_ref[...])
    own = (iota((TAPROWS, 896), 0) >> 2) == (iota((TAPROWS, 896), 1) >> 5)
    folded = jnp.sum(jnp.where(own, products, 0.0).reshape(TAPROWS // 8, 8, 896), axis=0)
    lifted = folded[:, 0:128]
    for at in range(128, 896, 128):
        lifted = lifted + folded[:, at : at + 128]
    lifted = lifted + pltpu.roll(lifted, 64, 1)
    lifted = lifted + pltpu.roll(lifted, 32, 1)
    lifted = lifted + pltpu.roll(lifted, 4, 0)
    lanes = iota((8, 128), 1)
    shared = jnp.zeros((8, 128), F32)
    for b in range(4):
        rows = moments[8 * b : 8 * b + 8]
        rows = rows if b == 0 else pltpu.roll(rows, 4 * b, 1)
        shared = jnp.where((lanes >= 108 + 4 * b) & (lanes < 112 + 4 * b), rows, shared)
    upper = iota((8, 128), 0) < 4
    for k in range(4):
        first = pltpu.roll(lifted, 124 - 8 * k, 1)
        second = pltpu.roll(lifted, 120 - 8 * k, 1)
        columns = jnp.where(upper, first, second)
        message = jnp.where(lanes < 108, moments[8 * k : 8 * k + 8], shared)
        message = jnp.where(lanes >= 124, columns, message).astype(send_ref.dtype)
        send_ref[k] = jnp.broadcast_to(message[None], send_ref.shape[1:])
    for item in out_copies:
        item.wait()


def finish_kernel(scale, inv, recv_ref, taps_ref, owned_ref, conv_out, mix_out, lift_out):
    flat = recv_ref[...].reshape(1024, 128)
    total = dot(ones_where(iota((8, 1024), 0) == (iota((8, 1024), 1) & 7)), flat)
    high, low = split(total)
    both = jnp.concatenate([high.astype(F32), low.astype(F32)], axis=0).astype(BF16)
    conv = dot(both, taps_ref[...], NT)
    conv_out[0] = (conv[:8] + conv[8:]) * scale
    mixed = dot(owned_ref[...], both, NT) * (scale * inv)
    for b in range(4):
        rows = mixed[8 * b : 8 * b + 8]
        mix_out[0, :, 8 * b : 8 * b + 8] = rows[:, :8] + rows[:, 8:]
    lift_out[:, 0:4] = total[0:4, 124:128] * scale
    lift_out[:, 4:8] = total[4:8, 124:128] * scale


VMEM = pl.BlockSpec(memory_space=pltpu.VMEM)
HBM = pl.BlockSpec(memory_space=pltpu.HBM)


def in_hbm(array):
    return pltpu.with_memory_space_constraint(array, pltpu.HBM)


LIMIT = pltpu.CompilerParams(vmem_limit_bytes=20 * 1024 * 1024)


def on_device(micro_fields, lift_w, conv_w, mix_w, phi, psi, cotangent):
    micro = micro_fields[0]
    rank = phi.shape[0]
    cells = micro.shape[1] * micro.shape[2] * micro.shape[3]
    gx, gy, reps = lax.axis_size("gx"), lax.axis_size("gy"), lax.axis_size("rep")
    total_cells = cells * gx * gy
    inv = 1.0 / math.sqrt(total_cells) / math.sqrt(rank)
    scale = 1.0 / math.sqrt(total_cells * reps)
    codes = jnp.asarray(stack_codes())

    even = lax.axis_index("gx") % 2 == 0
    first, last = micro[:, 0], micro[:, -1]
    on_chip = [(i, i ^ 1) for i in range(gx)]
    off_chip = [(i, ((i + 1) ^ 1) - 1) for i in range(1, gx - 1)]
    near = lax.ppermute(jnp.where(even, last, first), "gx", on_chip)
    far = lax.ppermute(jnp.where(even, first, last), "gx", off_chip)

    rows = (rank // 4, 3 * rank // 8, 3 * rank // 8)
    parts, *pieces = pl.pallas_call(
        functools.partial(project_kernel, rows),
        in_specs=[HBM] * 3,
        out_specs=[HBM] + [VMEM] * EARLY,
        out_shape=[jax.ShapeDtypeStruct((gx * gy, 32, 128), BF16)]
        + [jax.ShapeDtypeStruct((rank // PIECES,) + psi.shape[1:], BF16)] * EARLY,
        scratch_shapes=[
            pltpu.VMEM(micro.shape, BF16),
            pltpu.VMEM(phi.shape, BF16),
            pltpu.VMEM((4, 32, 128), F32),
            pltpu.VMEM((gx * gy, 32, 128), BF16),
            pltpu.SemaphoreType.DMA((len(rows) + 2 + EARLY,)),
        ],
        compiler_params=pltpu.CompilerParams(vmem_limit_bytes=16 * 1024 * 1024),
        name="project",
    )(in_hbm(micro), in_hbm(phi), in_hbm(psi))

    gathered = lax.all_to_all(parts, ("gx", "gy"), 0, 0)

    weights, pairs, taps, owned = pl.pallas_call(
        functools.partial(stage_kernel, inv),
        in_specs=[VMEM] * 3,
        out_specs=[VMEM] * 4,
        out_shape=[
            jax.ShapeDtypeStruct((32, TAPROWS), BF16),
            jax.ShapeDtypeStruct((64, 896), BF16),
            jax.ShapeDtypeStruct((864, 128), BF16),
            jax.ShapeDtypeStruct((32, 128), BF16),
        ],
        compiler_params=pltpu.CompilerParams(vmem_limit_bytes=8 * 1024 * 1024),
        cost_estimate=pl.CostEstimate(flops=2_000_000_000, bytes_accessed=4_000_000, transcendentals=0),
        name="stage",
    )(lift_w, conv_w, mix_w)

    out_shape = jax.ShapeDtypeStruct((1, 32, 4, 16, 128), F32)
    out_field, send = pl.pallas_call(
        main_kernel,
        in_specs=[VMEM] * (7 + EARLY) + [HBM] * 2,
        out_specs=[HBM, VMEM],
        out_shape=[out_shape, jax.ShapeDtypeStruct((reps, gx * gy, 8, 128), BF16)],
        scratch_shapes=[
            pltpu.VMEM((512, STACK), BF16),
            pltpu.VMEM((STACK, 512), BF16),
            pltpu.VMEM((128, 4096), BF16),
            pltpu.VMEM((512, 512), F32),
            pltpu.VMEM((512, 512), BF16),
            pltpu.VMEM((512, STACK), F32),
            pltpu.VMEM((rank // PIECES * (PIECES - EARLY),) + psi.shape[1:], BF16),
            pltpu.VMEM(cotangent.shape, BF16),
            pltpu.VMEM(out_shape.shape, F32),
            pltpu.SemaphoreType.DMA((PIECES - EARLY + 3,)),
        ],
        compiler_params=LIMIT,
        cost_estimate=pl.CostEstimate(flops=4_000_000_000, bytes_accessed=6_000_000, transcendentals=500_000),
        name="layer",
    )(gathered, micro, near, far, weights, pairs, codes, *pieces, in_hbm(psi), in_hbm(cotangent))

    received = lax.all_to_all(send.reshape(reps * gx * gy, 8, 128), ("rep", "gx", "gy"), 0, 0)

    grads = pl.pallas_call(
        functools.partial(finish_kernel, scale, inv),
        in_specs=[VMEM] * 3,
        out_specs=[VMEM] * 3,
        out_shape=[
            jax.ShapeDtypeStruct((1, 8, 864), F32),
            jax.ShapeDtypeStruct((1, 8, 32), F32),
            jax.ShapeDtypeStruct((4, 8), F32),
        ],
        compiler_params=LIMIT,
        name="finish",
    )(received, taps, owned)
    return (out_field, *grads)


def solution(mesh):
    return jax.shard_map(
        on_device,
        mesh=mesh,
        in_specs=(
            P("rep", None, "gx", "gy", None),
            P(),
            P(),
            P(),
            P(None, "gx", "gy", None),
            P(None, "gx", "gy", None),
            P("rep", None, "gx", "gy", None),
        ),
        out_specs=(
            P("rep", None, "gx", "gy", None),
            P(None, "rep", None),
            P(None, "rep", None),
            P(None, "rep"),
        ),
        check_vma=False,
    )
```

```python
import functools
import math

import jax
import jax.numpy as jnp
import numpy as np
from jax import lax
from jax.experimental import pallas as pl
from jax.experimental.pallas import tpu as pltpu
from jax.sharding import PartitionSpec as P

F32 = jnp.float32
BF16 = jnp.bfloat16
NN = (((1,), (0,)), ((), ()))
NT = (((1,), (1,)), ((), ()))
TN = (((0,), (0,)), ((), ()))

STACK = 768
HALO_AT = 576
U_AT = 704
PIECES = 8
EARLY = 5
TAPROWS = 128


ROLLED = HALO_AT


def stack_codes():
    codes = np.full((8, STACK), -1, np.int32)
    codes[3] = -100
    for lane in range(STACK):
        if lane < HALO_AT:
            group, row = divmod(lane, 16)
            dx, dz, j = group // 12, group // 4 % 3, group % 4
        elif lane < HALO_AT + 72:
            at = lane - HALO_AT
            dx, dz, side, j = at // 24, at // 8 % 3, at // 4 % 2, at % 4
            row = 16 if side else -1
        elif lane >= U_AT:
            j, row = divmod(lane - U_AT, 16)
            codes[1, lane] = codes[4, lane] = 108 + j
            codes[3, lane], codes[5, lane] = row, 0
            continue
        else:
            continue
        for dy in range(3):
            codes[dy, lane] = (9 * dx + 3 * dy + dz) * 4 + j
        codes[3, lane], codes[5, lane] = row, 1
        if lane >= HALO_AT:
            codes[4, lane] = codes[2 if side else 0, lane]
        elif 7 <= row < 10:
            codes[4, lane] = codes[row - 7, lane]
    return codes


def dot(a, b, dims=NN):
    return lax.dot_general(a, b, dims, preferred_element_type=F32)


def split(values):
    high = values.astype(BF16)
    return high, (values - high.astype(F32)).astype(BF16)


def dot_split(a, b, dims=NN):
    high, low = split(a)
    return dot(high, b, dims) + dot(low, b, dims)


def iota(shape, dim):
    return lax.broadcasted_iota(jnp.int32, shape, dim)


def ones_where(condition):
    return jnp.where(condition, 1.0, 0.0).astype(BF16)


def row_sums(tiles):
    rows = iota((8, 128), 0)
    for step in (1, 2, 4):
        first = (rows & step) == 0
        tiles = [
            jnp.where(first, a, b) + pltpu.roll(jnp.where(first, b, a), 8 - step, 0)
            for a, b in zip(tiles[0::2], tiles[1::2])
        ]
    return tiles[0]


def selector(codes, dy):
    return ones_where(iota((TAPROWS, STACK), 0) == codes[dy : dy + 1, :])


def band(codes, dy):
    return (codes[3:4, :] - iota((16, STACK), 0)) == dy - 1


def lift_columns(lift, first):
    rows = iota((4, 128), 0)
    lanes = iota((4, 128), 1)
    if first is None:
        pick = ((lanes & 3) == rows) & (lanes < 108)
    else:
        pick = (lanes - first) == rows
    return dot(lift, ones_where(pick), TN)


def lift_blocks(lift):
    columns = lift_columns(lift, None)
    own = iota((27, 1, 128), 0) == (iota((27, 1, 128), 2) >> 2)
    return jnp.where(own, columns[None], 0.0).reshape(864, 128).astype(BF16)


def weight_table(weights, codes, table):
    spread = dot(weights, selector(codes, 4))
    valid = jnp.abs(codes[3:4, :] - iota((16, STACK), 0)) <= codes[5:6, :]
    for o in range(32):
        for at in range(0, STACK, 128):
            lanes = slice(at, at + 128)
            whole = jnp.broadcast_to(spread[o : o + 1, lanes], (16, 128))
            if at < ROLLED:
                rolled = pltpu.roll(whole, 120, 1, stride=1, stride_axis=0)
                if at + 128 > ROLLED:
                    rolled = jnp.where(iota((16, 128), 1) < ROLLED - at, rolled, whole)
                whole = rolled
            table[16 * o : 16 * o + 16, lanes] = jnp.where(valid[:, lanes], whole, 0.0).astype(BF16)


def stage_kernel(inv, lift_ref, conv_ref, mix_ref, weights_ref, pairs_ref, taps_ref, owned_ref):
    lift, conv, mix = lift_ref[...], conv_ref[0], mix_ref[0]
    blocks = lift_blocks(lift)
    taps_ref[...] = blocks
    own_lift = lift_columns(lift, 108)
    mixed = dot(mix, own_lift.astype(BF16), TN) * inv
    weights_ref[...] = (dot(conv, blocks) + mixed).astype(BF16)
    eye = ones_where(iota((32, 32), 0) == iota((32, 32), 1))
    turned = (dot(eye, mix, NT) * inv).astype(BF16)
    pairs = jnp.concatenate([conv, turned], axis=1)
    pairs_ref[...] = jnp.concatenate([pairs, pairs], axis=0)
    rep = lax.axis_index("rep")
    pick = ones_where(iota((8, 32), 1) == iota((8, 32), 0) + 8 * rep)
    mine = dot(pick, own_lift.astype(BF16))
    owned_ref[...] = jnp.concatenate(
        [mine if b == 0 else pltpu.roll(mine, 4 * b, 1) for b in range(4)], axis=0
    ).astype(BF16)


def project_kernel(parts, micro_ref, phi_ref, psi_ref, out_ref, *rest):
    pieces, (fields_ref, basis_ref, sums, message, sems) = rest[:EARLY], rest[EARLY:]

    def copy(at, count, sem):
        rows = pl.ds(at, count)
        return pltpu.make_async_copy(phi_ref.at[rows], basis_ref.at[rows], sem)

    starts = [sum(parts[:k]) for k in range(len(parts))]
    copies = [copy(at, count, sems.at[k]) for k, (at, count) in enumerate(zip(starts, parts))]
    own = pltpu.make_async_copy(micro_ref, fields_ref, sems.at[len(parts)])
    own.start()
    for item in copies:
        item.start()
    count = psi_ref.shape[0] // PIECES
    others = [
        pltpu.make_async_copy(
            psi_ref.at[pl.ds(k * count, count)], piece, sems.at[len(parts) + 2 + k]
        )
        for k, piece in enumerate(pieces)
    ]
    own.wait()
    fields = jnp.concatenate([fields_ref[:, x].reshape(64, 128) for x in range(4)], axis=1)
    me = lax.axis_index("gy")
    upper = iota((8, 128), 0) < 4
    edges = []
    for row in (0, 15):
        pick = ones_where(iota((8, 64), 1) == (iota((8, 64), 0) & 3) * 16 + row)
        edge = dot(pick, fields)
        halves = [
            jnp.where(upper, edge[:, at : at + 128], edge[:, at + 128 : at + 256]) for at in (0, 256)
        ]
        edges.append(jnp.concatenate(halves, axis=0))
    rims = [jnp.where(target > me, edges[1], edges[0]) for target in range(4)]
    for item, at, count in zip(copies, starts, parts):
        item.wait()
        if at == starts[1]:
            for other in others:
                other.start()
        wide = count * 16
        basis = jnp.concatenate(
            [basis_ref[at : at + count, x].reshape(wide, 128) for x in range(4)], axis=1
        )
        product = dot(fields, basis, NT)
        same = iota((16, 128), 0) == (iota((16, 128), 1) & 15)
        for chunk in range(0, count // 8, 4):
            row = at // 8 + chunk
            for pair in (0, 2):
                tiles = []
                for j in (pair, pair + 1):
                    for one in range(chunk, chunk + 4):
                        block = product[16 * j : 16 * j + 16, 128 * one : 128 * one + 128]
                        block = jnp.where(same, block, 0.0)
                        tiles.append(block[:8] + block[8:])
                packed = row_sums(tiles)
                sums[pair, row : row + 4, :] = packed[:4]
                sums[pair + 1, row : row + 4, :] = packed[4:]
    groups = ones_where(iota((8, 128), 0) == (iota((8, 128), 1) >> 4))
    first_part, rest = split(sums[...].reshape(128, 128))
    total = dot(groups, first_part, NT) + dot(groups, rest, NT)
    high = total.astype(BF16).astype(F32)
    for target in range(4):
        whole = jnp.concatenate([high, total - high, rims[target]], axis=0).astype(BF16)
        for plane in range(message.shape[0] // 4):
            message[4 * plane + target] = whole
    send = pltpu.make_async_copy(message, out_ref, sems.at[len(parts) + 1])
    send.start()
    for other in others:
        other.wait()
    send.wait()


def shift_z(values, dz):
    if dz == 0:
        return values
    lanes = iota(values.shape, 1) & 127
    width = values.shape[1]
    pieces = [
        pltpu.roll(values[:, at : at + 128], (-dz) % 128, 1) for at in range(0, width, 128)
    ]
    rolled = jnp.concatenate(pieces, axis=1)
    return jnp.where(lanes == (127 if dz > 0 else 0), 0.0, rolled)


def received_rims(parts_ref):
    gx, gy = lax.axis_index("gx"), lax.axis_index("gy")
    planes = parts_ref.shape[0] // 4

    def tile(plane, row, at):
        valid = (plane >= 0) & (plane < planes) & (row >= 0) & (row < 4)
        peer = jnp.clip(plane, 0, planes - 1) * 4 + jnp.clip(row, 0, 3)
        both = parts_ref[peer, 16:32, :].astype(F32)
        return jnp.where(valid, both[at : at + 8], 0.0)

    pieces = []
    lower = iota((8, 128), 0) < 4
    for x in range(6):
        plane = gx - 1 if x == 0 else gx + 1 if x == 5 else gx
        own = (x - 1) % 4
        below, above = [tile(plane, gy + step, 8 * (own // 2)) for step in (-1, 1)]
        if own % 2:
            below = pltpu.roll(below, 4, 0)
        else:
            above = pltpu.roll(above, 4, 0)
        pieces.append(jnp.where(lower, below, above))
    return jnp.concatenate(pieces, axis=1)


def main_kernel(parts_ref, micro_ref, near_ref, far_ref, weights_ref, pairs_ref, codes_ref, *rest):
    psi_refs = list(rest[:EARLY])
    psi_ref, cot_ref, out_ref, send_ref = rest[EARLY : EARLY + 4]
    table, stack, spread, pre, grad, corr, late_ref, cot, out, sems = rest[EARLY + 4 :]
    count = psi_ref.shape[0] // PIECES
    late = PIECES - EARLY
    copies = []
    for k in range(late):
        piece = late_ref.at[pl.ds(k * count, count)]
        copies.append(
            pltpu.make_async_copy(psi_ref.at[pl.ds((EARLY + k) * count, count)], piece, sems.at[k])
        )
        psi_refs.append(piece)
    cot_copy = pltpu.make_async_copy(cot_ref, cot, sems.at[late])
    for item in copies + [cot_copy]:
        item.start()
    codes = codes_ref[...]
    weight_table(weights_ref[...], codes, table)
    even = lax.axis_index("gx") % 2 == 0
    near, far = near_ref[...], far_ref[...]
    ends = jnp.where(even, far, near), jnp.where(even, near, far)
    planes = [ends[0]] + [micro_ref[:, x] for x in range(4)] + [ends[1]]
    fields = jnp.concatenate([plane.reshape(64, 128) for plane in planes], axis=1).astype(F32)
    rims = received_rims(parts_ref)
    rim_rows = {}
    for dz in range(3):
        moved = shift_z(fields, dz - 1).astype(BF16)
        moved_rim = shift_z(rims, dz - 1)
        for dx in range(3):
            at = (dx * 3 + dz) * 64
            stack[at : at + 64, :] = moved[:, 128 * dx : 128 * dx + 512]
            rim_rows[dx, dz] = moved_rim[:, 128 * dx : 128 * dx + 512]
    rim_block = jnp.concatenate([rim_rows[dx, dz] for dx in range(3) for dz in range(3)], axis=0)
    stack[HALO_AT:U_AT, :] = jnp.concatenate(
        [rim_block, jnp.zeros((U_AT - HALO_AT - 72, 512), F32)], axis=0
    ).astype(BF16)
    both = jnp.sum(parts_ref[:, 0:16, :].astype(F32), axis=0)
    high, low = split(both[:8] + both[8:])
    groups = ones_where(iota((8, 128), 0) == (iota((8, 128), 1) >> 4))
    same = iota((16, 128), 0) == (iota((16, 128), 1) & 15)
    for part, values in enumerate((high, low)):
        expanded = dot(values, groups, TN)
        for j in range(4):
            for chunk in range(32):
                row = expanded[32 * j + chunk : 32 * j + chunk + 1, :]
                at = 64 * part + 16 * j
                spread[at : at + 16, 128 * chunk : 128 * chunk + 128] = jnp.where(
                    same, row, 0.0
                ).astype(BF16)
    fields = [jnp.zeros((128, 256), F32) for _ in range(2)]
    for k, piece in enumerate(psi_refs):
        if k == EARLY:
            for item in copies:
                item.wait()
        for pair in range(2):
            for row in range(0, count, 16):
                at = k * count + row
                basis = jnp.concatenate(
                    [piece[row : row + 16, 2 * pair + n].reshape(256, 128) for n in range(2)], axis=1
                )
                fields[pair] = fields[pair] + dot(spread[:, 16 * at : 16 * at + 256], basis)
    for pair, field in enumerate(fields):
        stack[U_AT:STACK, 256 * pair : 256 * pair + 256] = (field[:64] + field[64:]).astype(BF16)
    cot_copy.wait()
    out_copies = []
    for pair in range(2):
        half = slice(256 * pair, 256 * pair + 256)
        pre[:, half] = dot(table[...], stack[:, half])
        for o in range(32):
            rows = slice(16 * o, 16 * o + 16)
            for x in (2 * pair, 2 * pair + 1):
                lanes = slice(128 * x, 128 * x + 128)
                values = pre[rows, lanes]
                cumulative = 0.5 * (1.0 + lax.erf(values * (1.0 / math.sqrt(2.0))))
                density = jnp.exp(-0.5 * values * values) * (1.0 / math.sqrt(2.0 * math.pi))
                out[0, o, x] = values * cumulative
                slope = cumulative + values * density
                grad[rows, lanes] = (cot[0, o, x].astype(F32) * slope).astype(BF16)
        out_copies.append(
            pltpu.make_async_copy(
                out.at[:, :, pl.ds(2 * pair, 2)], out_ref.at[:, :, pl.ds(2 * pair, 2)], sems.at[late + 1 + pair]
            )
        )
        out_copies[-1].start()
        product = dot(grad[:, half], stack[:, half], NT)
        if pair == 0:
            corr[...] = product
        else:
            corr[...] += product
    moments = jnp.zeros((32, TAPROWS), F32)
    for dy in range(3):
        valid = band(codes, dy)
        reduced = []
        for first in range(0, 32, 8):
            pieces = []
            for at in range(0, STACK, 128):
                lanes = slice(at, at + 128)
                tiles = []
                for o in range(first, first + 8):
                    block = jnp.where(valid[:, lanes], corr[16 * o : 16 * o + 16, lanes], 0.0)
                    tiles.append(block[:8] + block[8:])
                pieces.append(row_sums(tiles))
            reduced.append(jnp.concatenate(pieces, axis=1))
        moments = moments + dot_split(jnp.concatenate(reduced, axis=0), selector(codes, dy), NT)
    turned_high, turned_low = split(moments.T)
    turned = jnp.concatenate([turned_high, turned_low], axis=1)
    products = dot(turned, pairs_ref[...])
    own = (iota((TAPROWS, 896), 0) >> 2) == (iota((TAPROWS, 896), 1) >> 5)
    folded = jnp.sum(jnp.where(own, products, 0.0).reshape(TAPROWS // 8, 8, 896), axis=0)
    lifted = folded[:, 0:128]
    for at in range(128, 896, 128):
        lifted = lifted + folded[:, at : at + 128]
    lifted = lifted + pltpu.roll(lifted, 64, 1)
    lifted = lifted + pltpu.roll(lifted, 32, 1)
    lifted = lifted + pltpu.roll(lifted, 4, 0)
    lanes = iota((8, 128), 1)
    shared = jnp.zeros((8, 128), F32)
    for b in range(4):
        rows = moments[8 * b : 8 * b + 8]
        rows = rows if b == 0 else pltpu.roll(rows, 4 * b, 1)
        shared = jnp.where((lanes >= 108 + 4 * b) & (lanes < 112 + 4 * b), rows, shared)
    upper = iota((8, 128), 0) < 4
    for k in range(4):
        first = pltpu.roll(lifted, 124 - 8 * k, 1)
        second = pltpu.roll(lifted, 120 - 8 * k, 1)
        columns = jnp.where(upper, first, second)
        message = jnp.where(lanes < 108, moments[8 * k : 8 * k + 8], shared)
        message = jnp.where(lanes >= 124, columns, message).astype(send_ref.dtype)
        send_ref[k] = jnp.broadcast_to(message[None], send_ref.shape[1:])
    for item in out_copies:
        item.wait()


def finish_kernel(scale, inv, recv_ref, taps_ref, owned_ref, conv_out, mix_out, lift_out):
    flat = recv_ref[...].reshape(1024, 128)
    total = dot(ones_where(iota((8, 1024), 0) == (iota((8, 1024), 1) & 7)), flat)
    high, low = split(total)
    both = jnp.concatenate([high.astype(F32), low.astype(F32)], axis=0).astype(BF16)
    conv = dot(both, taps_ref[...], NT)
    conv_out[0] = (conv[:8] + conv[8:]) * scale
    mixed = dot(owned_ref[...], both, NT) * (scale * inv)
    for b in range(4):
        rows = mixed[8 * b : 8 * b + 8]
        mix_out[0, :, 8 * b : 8 * b + 8] = rows[:, :8] + rows[:, 8:]
    lift_out[:, 0:4] = total[0:4, 124:128] * scale
    lift_out[:, 4:8] = total[4:8, 124:128] * scale


VMEM = pl.BlockSpec(memory_space=pltpu.VMEM)
HBM = pl.BlockSpec(memory_space=pltpu.HBM)


def in_hbm(array):
    return pltpu.with_memory_space_constraint(array, pltpu.HBM)


LIMIT = pltpu.CompilerParams(vmem_limit_bytes=20 * 1024 * 1024)


def on_device(micro_fields, lift_w, conv_w, mix_w, phi, psi, cotangent):
    micro = micro_fields[0]
    rank = phi.shape[0]
    cells = micro.shape[1] * micro.shape[2] * micro.shape[3]
    gx, gy, reps = lax.axis_size("gx"), lax.axis_size("gy"), lax.axis_size("rep")
    total_cells = cells * gx * gy
    inv = 1.0 / math.sqrt(total_cells) / math.sqrt(rank)
    scale = 1.0 / math.sqrt(total_cells * reps)
    codes = jnp.asarray(stack_codes())

    even = lax.axis_index("gx") % 2 == 0
    first, last = micro[:, 0], micro[:, -1]
    on_chip = [(i, i ^ 1) for i in range(gx)]
    off_chip = [(i, ((i + 1) ^ 1) - 1) for i in range(1, gx - 1)]
    near = lax.ppermute(jnp.where(even, last, first), "gx", on_chip)
    far = lax.ppermute(jnp.where(even, first, last), "gx", off_chip)

    rows = (rank // 4, 3 * rank // 8, 3 * rank // 8)
    parts, *pieces = pl.pallas_call(
        functools.partial(project_kernel, rows),
        in_specs=[HBM] * 3,
        out_specs=[HBM] + [VMEM] * EARLY,
        out_shape=[jax.ShapeDtypeStruct((gx * gy, 32, 128), BF16)]
        + [jax.ShapeDtypeStruct((rank // PIECES,) + psi.shape[1:], BF16)] * EARLY,
        scratch_shapes=[
            pltpu.VMEM(micro.shape, BF16),
            pltpu.VMEM(phi.shape, BF16),
            pltpu.VMEM((4, 32, 128), F32),
            pltpu.VMEM((gx * gy, 32, 128), BF16),
            pltpu.SemaphoreType.DMA((len(rows) + 2 + EARLY,)),
        ],
        compiler_params=pltpu.CompilerParams(vmem_limit_bytes=16 * 1024 * 1024),
        name="project",
    )(in_hbm(micro), in_hbm(phi), in_hbm(psi))

    gathered = lax.all_to_all(parts, ("gx", "gy"), 0, 0)

    weights, pairs, taps, owned = pl.pallas_call(
        functools.partial(stage_kernel, inv),
        in_specs=[VMEM] * 3,
        out_specs=[VMEM] * 4,
        out_shape=[
            jax.ShapeDtypeStruct((32, TAPROWS), BF16),
            jax.ShapeDtypeStruct((64, 896), BF16),
            jax.ShapeDtypeStruct((864, 128), BF16),
            jax.ShapeDtypeStruct((32, 128), BF16),
        ],
        compiler_params=pltpu.CompilerParams(vmem_limit_bytes=8 * 1024 * 1024),
        cost_estimate=pl.CostEstimate(flops=2_000_000_000, bytes_accessed=4_000_000, transcendentals=0),
        name="stage",
    )(lift_w, conv_w, mix_w)

    out_shape = jax.ShapeDtypeStruct((1, 32, 4, 16, 128), F32)
    out_field, send = pl.pallas_call(
        main_kernel,
        in_specs=[VMEM] * (7 + EARLY) + [HBM] * 2,
        out_specs=[HBM, VMEM],
        out_shape=[out_shape, jax.ShapeDtypeStruct((reps, gx * gy, 8, 128), BF16)],
        scratch_shapes=[
            pltpu.VMEM((512, STACK), BF16),
            pltpu.VMEM((STACK, 512), BF16),
            pltpu.VMEM((128, 4096), BF16),
            pltpu.VMEM((512, 512), F32),
            pltpu.VMEM((512, 512), BF16),
            pltpu.VMEM((512, STACK), F32),
            pltpu.VMEM((rank // PIECES * (PIECES - EARLY),) + psi.shape[1:], BF16),
            pltpu.VMEM(cotangent.shape, BF16),
            pltpu.VMEM(out_shape.shape, F32),
            pltpu.SemaphoreType.DMA((PIECES - EARLY + 3,)),
        ],
        compiler_params=LIMIT,
        cost_estimate=pl.CostEstimate(flops=4_000_000_000, bytes_accessed=6_000_000, transcendentals=500_000),
        name="layer",
    )(gathered, micro, near, far, weights, pairs, codes, *pieces, in_hbm(psi), in_hbm(cotangent))

    received = lax.all_to_all(send.reshape(reps * gx * gy, 8, 128), ("rep", "gx", "gy"), 0, 0)

    grads = pl.pallas_call(
        functools.partial(finish_kernel, scale, inv),
        in_specs=[VMEM] * 3,
        out_specs=[VMEM] * 3,
        out_shape=[
            jax.ShapeDtypeStruct((1, 8, 864), F32),
            jax.ShapeDtypeStruct((1, 8, 32), F32),
            jax.ShapeDtypeStruct((4, 8), F32),
        ],
        compiler_params=LIMIT,
        name="finish",
    )(received, taps, owned)
    return (out_field, *grads)


def solution(mesh):
    return jax.shard_map(
        on_device,
        mesh=mesh,
        in_specs=(
            P("rep", None, "gx", "gy", None),
            P(),
            P(),
            P(),
            P(None, "gx", "gy", None),
            P(None, "gx", "gy", None),
            P("rep", None, "gx", "gy", None),
        ),
        out_specs=(
            P("rep", None, "gx", "gy", None),
            P(None, "rep", None),
            P(None, "rep", None),
            P(None, "rep"),
        ),
        check_vma=False,
    )
```

```python
import functools
import math

import jax
import jax.numpy as jnp
import numpy as np
from jax import lax
from jax.experimental import pallas as pl
from jax.experimental.pallas import tpu as pltpu
from jax.sharding import PartitionSpec as P

F32 = jnp.float32
BF16 = jnp.bfloat16
NN = (((1,), (0,)), ((), ()))
NT = (((1,), (1,)), ((), ()))
TN = (((0,), (0,)), ((), ()))

STACK = 768
HALO_AT = 576
U_AT = 704
PIECES = 8
EARLY = 5
TAPROWS = 128


ROLLED = HALO_AT


def stack_codes():
    codes = np.full((8, STACK), -1, np.int32)
    codes[3] = -100
    for lane in range(STACK):
        if lane < HALO_AT:
            group, row = divmod(lane, 16)
            dx, dz, j = group // 12, group // 4 % 3, group % 4
        elif lane < HALO_AT + 72:
            at = lane - HALO_AT
            dx, dz, side, j = at // 24, at // 8 % 3, at // 4 % 2, at % 4
            row = 16 if side else -1
        elif lane >= U_AT:
            j, row = divmod(lane - U_AT, 16)
            codes[1, lane] = codes[4, lane] = 108 + j
            codes[3, lane], codes[5, lane] = row, 0
            continue
        else:
            continue
        for dy in range(3):
            codes[dy, lane] = (9 * dx + 3 * dy + dz) * 4 + j
        codes[3, lane], codes[5, lane] = row, 1
        if lane >= HALO_AT:
            codes[4, lane] = codes[2 if side else 0, lane]
        elif 7 <= row < 10:
            codes[4, lane] = codes[row - 7, lane]
    return codes


def dot(a, b, dims=NN):
    return lax.dot_general(a, b, dims, preferred_element_type=F32)


def split(values):
    high = values.astype(BF16)
    return high, (values - high.astype(F32)).astype(BF16)


def dot_split(a, b, dims=NN):
    high, low = split(a)
    return dot(high, b, dims) + dot(low, b, dims)


def iota(shape, dim):
    return lax.broadcasted_iota(jnp.int32, shape, dim)


def ones_where(condition):
    return jnp.where(condition, 1.0, 0.0).astype(BF16)


def row_sums(tiles):
    rows = iota((8, 128), 0)
    for step in (1, 2, 4):
        first = (rows & step) == 0
        tiles = [
            jnp.where(first, a, b) + pltpu.roll(jnp.where(first, b, a), 8 - step, 0)
            for a, b in zip(tiles[0::2], tiles[1::2])
        ]
    return tiles[0]


def selector(codes, dy):
    return ones_where(iota((TAPROWS, STACK), 0) == codes[dy : dy + 1, :])


def band(codes, dy):
    return (codes[3:4, :] - iota((16, STACK), 0)) == dy - 1


def lift_columns(lift, first):
    rows = iota((4, 128), 0)
    lanes = iota((4, 128), 1)
    if first is None:
        pick = ((lanes & 3) == rows) & (lanes < 108)
    else:
        pick = (lanes - first) == rows
    return dot(lift, ones_where(pick), TN)


def lift_blocks(lift):
    columns = lift_columns(lift, None)
    own = iota((27, 1, 128), 0) == (iota((27, 1, 128), 2) >> 2)
    return jnp.where(own, columns[None], 0.0).reshape(864, 128).astype(BF16)


def weight_table(weights, codes, table):
    spread = dot(weights, selector(codes, 4))
    valid = jnp.abs(codes[3:4, :] - iota((16, STACK), 0)) <= codes[5:6, :]
    for o in range(32):
        for at in range(0, STACK, 128):
            lanes = slice(at, at + 128)
            whole = jnp.broadcast_to(spread[o : o + 1, lanes], (16, 128))
            if at < ROLLED:
                rolled = pltpu.roll(whole, 120, 1, stride=1, stride_axis=0)
                if at + 128 > ROLLED:
                    rolled = jnp.where(iota((16, 128), 1) < ROLLED - at, rolled, whole)
                whole = rolled
            table[16 * o : 16 * o + 16, lanes] = jnp.where(valid[:, lanes], whole, 0.0).astype(BF16)


def stage_kernel(inv, lift_ref, conv_ref, mix_ref, weights_ref, pairs_ref, taps_ref, owned_ref):
    lift, conv, mix = lift_ref[...], conv_ref[0], mix_ref[0]
    blocks = lift_blocks(lift)
    taps_ref[...] = blocks
    own_lift = lift_columns(lift, 108)
    mixed = dot(mix, own_lift.astype(BF16), TN) * inv
    weights_ref[...] = (dot(conv, blocks) + mixed).astype(BF16)
    eye = ones_where(iota((32, 32), 0) == iota((32, 32), 1))
    turned = (dot(eye, mix, NT) * inv).astype(BF16)
    pairs = jnp.concatenate([conv, turned], axis=1)
    pairs_ref[...] = jnp.concatenate([pairs, pairs], axis=0)
    rep = lax.axis_index("rep")
    pick = ones_where(iota((8, 32), 1) == iota((8, 32), 0) + 8 * rep)
    mine = dot(pick, own_lift.astype(BF16))
    owned_ref[...] = jnp.concatenate(
        [mine if b == 0 else pltpu.roll(mine, 4 * b, 1) for b in range(4)], axis=0
    ).astype(BF16)


def project_kernel(parts, micro_ref, phi_ref, psi_ref, out_ref, *rest):
    pieces, (fields_ref, basis_ref, sums, message, sems) = rest[:EARLY], rest[EARLY:]

    def copy(at, count, sem):
        rows = pl.ds(at, count)
        return pltpu.make_async_copy(phi_ref.at[rows], basis_ref.at[rows], sem)

    starts = [sum(parts[:k]) for k in range(len(parts))]
    copies = [copy(at, count, sems.at[k]) for k, (at, count) in enumerate(zip(starts, parts))]
    own = pltpu.make_async_copy(micro_ref, fields_ref, sems.at[len(parts)])
    own.start()
    for item in copies:
        item.start()
    count = psi_ref.shape[0] // PIECES
    others = [
        pltpu.make_async_copy(
            psi_ref.at[pl.ds(k * count, count)], piece, sems.at[len(parts) + 2 + k]
        )
        for k, piece in enumerate(pieces)
    ]
    own.wait()
    fields = jnp.concatenate([fields_ref[:, x].reshape(64, 128) for x in range(4)], axis=1)
    me = lax.axis_index("gy")
    upper = iota((8, 128), 0) < 4
    edges = []
    for row in (0, 15):
        pick = ones_where(iota((8, 64), 1) == (iota((8, 64), 0) & 3) * 16 + row)
        edge = dot(pick, fields)
        halves = [
            jnp.where(upper, edge[:, at : at + 128], edge[:, at + 128 : at + 256]) for at in (0, 256)
        ]
        edges.append(jnp.concatenate(halves, axis=0))
    rims = [jnp.where(target > me, edges[1], edges[0]) for target in range(4)]
    for item, at, count in zip(copies, starts, parts):
        item.wait()
        if at == starts[1]:
            for other in others:
                other.start()
        wide = count * 16
        basis = jnp.concatenate(
            [basis_ref[at : at + count, x].reshape(wide, 128) for x in range(4)], axis=1
        )
        product = dot(fields, basis, NT)
        same = iota((16, 128), 0) == (iota((16, 128), 1) & 15)
        for chunk in range(0, count // 8, 4):
            row = at // 8 + chunk
            for pair in (0, 2):
                tiles = []
                for j in (pair, pair + 1):
                    for one in range(chunk, chunk + 4):
                        block = product[16 * j : 16 * j + 16, 128 * one : 128 * one + 128]
                        block = jnp.where(same, block, 0.0)
                        tiles.append(block[:8] + block[8:])
                packed = row_sums(tiles)
                sums[pair, row : row + 4, :] = packed[:4]
                sums[pair + 1, row : row + 4, :] = packed[4:]
    groups = ones_where(iota((8, 128), 0) == (iota((8, 128), 1) >> 4))
    first_part, rest = split(sums[...].reshape(128, 128))
    total = dot(groups, first_part, NT) + dot(groups, rest, NT)
    high = total.astype(BF16).astype(F32)
    for target in range(4):
        whole = jnp.concatenate([high, total - high, rims[target]], axis=0).astype(BF16)
        for plane in range(message.shape[0] // 4):
            message[4 * plane + target] = whole
    send = pltpu.make_async_copy(message, out_ref, sems.at[len(parts) + 1])
    send.start()
    for other in others:
        other.wait()
    send.wait()


def shift_z(values, dz):
    if dz == 0:
        return values
    lanes = iota(values.shape, 1) & 127
    width = values.shape[1]
    pieces = [
        pltpu.roll(values[:, at : at + 128], (-dz) % 128, 1) for at in range(0, width, 128)
    ]
    rolled = jnp.concatenate(pieces, axis=1)
    return jnp.where(lanes == (127 if dz > 0 else 0), 0.0, rolled)


def received_rims(parts_ref):
    gx, gy = lax.axis_index("gx"), lax.axis_index("gy")
    planes = parts_ref.shape[0] // 4

    def tile(plane, row, at):
        valid = (plane >= 0) & (plane < planes) & (row >= 0) & (row < 4)
        peer = jnp.clip(plane, 0, planes - 1) * 4 + jnp.clip(row, 0, 3)
        both = parts_ref[peer, 16:32, :].astype(F32)
        return jnp.where(valid, both[at : at + 8], 0.0)

    pieces = []
    lower = iota((8, 128), 0) < 4
    for x in range(6):
        plane = gx - 1 if x == 0 else gx + 1 if x == 5 else gx
        own = (x - 1) % 4
        below, above = [tile(plane, gy + step, 8 * (own // 2)) for step in (-1, 1)]
        if own % 2:
            below = pltpu.roll(below, 4, 0)
        else:
            above = pltpu.roll(above, 4, 0)
        pieces.append(jnp.where(lower, below, above))
    return jnp.concatenate(pieces, axis=1)


def main_kernel(parts_ref, micro_ref, near_ref, far_ref, weights_ref, pairs_ref, codes_ref, *rest):
    psi_refs = list(rest[:EARLY])
    psi_ref, cot_ref, out_ref, send_ref = rest[EARLY : EARLY + 4]
    table, stack, spread, pre, grad, corr, late_ref, cot, out, sems = rest[EARLY + 4 :]
    count = psi_ref.shape[0] // PIECES
    late = PIECES - EARLY
    copies = []
    for k in range(late):
        piece = late_ref.at[pl.ds(k * count, count)]
        copies.append(
            pltpu.make_async_copy(psi_ref.at[pl.ds((EARLY + k) * count, count)], piece, sems.at[k])
        )
        psi_refs.append(piece)
    cot_copy = pltpu.make_async_copy(cot_ref, cot, sems.at[late])
    for item in copies:
        item.start()
    codes = codes_ref[...]
    weight_table(weights_ref[...], codes, table)
    even = lax.axis_index("gx") % 2 == 0
    near, far = near_ref[...], far_ref[...]
    ends = jnp.where(even, far, near), jnp.where(even, near, far)
    planes = [ends[0]] + [micro_ref[:, x] for x in range(4)] + [ends[1]]
    fields = jnp.concatenate([plane.reshape(64, 128) for plane in planes], axis=1).astype(F32)
    rims = received_rims(parts_ref)
    rim_rows = {}
    for dz in range(3):
        moved = shift_z(fields, dz - 1).astype(BF16)
        moved_rim = shift_z(rims, dz - 1)
        for dx in range(3):
            at = (dx * 3 + dz) * 64
            stack[at : at + 64, :] = moved[:, 128 * dx : 128 * dx + 512]
            rim_rows[dx, dz] = moved_rim[:, 128 * dx : 128 * dx + 512]
    rim_block = jnp.concatenate([rim_rows[dx, dz] for dx in range(3) for dz in range(3)], axis=0)
    stack[HALO_AT:U_AT, :] = jnp.concatenate(
        [rim_block, jnp.zeros((U_AT - HALO_AT - 72, 512), F32)], axis=0
    ).astype(BF16)
    cot_copy.start()
    both = jnp.sum(parts_ref[:, 0:16, :].astype(F32), axis=0)
    high, low = split(both[:8] + both[8:])
    groups = ones_where(iota((8, 128), 0) == (iota((8, 128), 1) >> 4))
    same = iota((16, 128), 0) == (iota((16, 128), 1) & 15)
    for part, values in enumerate((high, low)):
        expanded = dot(values, groups, TN)
        for j in range(4):
            for chunk in range(32):
                row = expanded[32 * j + chunk : 32 * j + chunk + 1, :]
                at = 64 * part + 16 * j
                spread[at : at + 16, 128 * chunk : 128 * chunk + 128] = jnp.where(
                    same, row, 0.0
                ).astype(BF16)
    fields = [jnp.zeros((128, 256), F32) for _ in range(2)]
    for k, piece in enumerate(psi_refs):
        if k == EARLY:
            for item in copies:
                item.wait()
        for pair in range(2):
            for row in range(0, count, 16):
                at = k * count + row
                basis = jnp.concatenate(
                    [piece[row : row + 16, 2 * pair + n].reshape(256, 128) for n in range(2)], axis=1
                )
                fields[pair] = fields[pair] + dot(spread[:, 16 * at : 16 * at + 256], basis)
    for pair, field in enumerate(fields):
        stack[U_AT:STACK, 256 * pair : 256 * pair + 256] = (field[:64] + field[64:]).astype(BF16)
    cot_copy.wait()
    out_copies = []
    for pair in range(2):
        half = slice(256 * pair, 256 * pair + 256)
        pre[:, half] = dot(table[...], stack[:, half])
        for o in range(32):
            rows = slice(16 * o, 16 * o + 16)
            for x in (2 * pair, 2 * pair + 1):
                lanes = slice(128 * x, 128 * x + 128)
                values = pre[rows, lanes]
                cumulative = 0.5 * (1.0 + lax.erf(values * (1.0 / math.sqrt(2.0))))
                density = jnp.exp(-0.5 * values * values) * (1.0 / math.sqrt(2.0 * math.pi))
                out[0, o, x] = values * cumulative
                slope = cumulative + values * density
                grad[rows, lanes] = (cot[0, o, x].astype(F32) * slope).astype(BF16)
        out_copies.append(
            pltpu.make_async_copy(
                out.at[:, :, pl.ds(2 * pair, 2)], out_ref.at[:, :, pl.ds(2 * pair, 2)], sems.at[late + 1 + pair]
            )
        )
        out_copies[-1].start()
        product = dot(grad[:, half], stack[:, half], NT)
        if pair == 0:
            corr[...] = product
        else:
            corr[...] += product
    bands = []
    for dy in range(3):
        valid = band(codes, dy)
        reduced = []
        for first in range(0, 32, 8):
            pieces = []
            for at in range(0, STACK, 128):
                lanes = slice(at, at + 128)
                tiles = []
                for o in range(first, first + 8):
                    block = jnp.where(valid[:, lanes], corr[16 * o : 16 * o + 16, lanes], 0.0)
                    tiles.append(block[:8] + block[8:])
                pieces.append(row_sums(tiles))
            reduced.append(jnp.concatenate(pieces, axis=1))
        bands.append(jnp.concatenate(reduced, axis=0))
    banded = jnp.concatenate(bands, axis=1)
    picks = jnp.concatenate([selector(codes, dy) for dy in range(3)], axis=1)
    high, low = split(banded)
    both = dot(jnp.concatenate([high, low], axis=0), picks, NT)
    moments = both[:32] + both[32:]
    turned_high, turned_low = split(moments.T)
    turned = jnp.concatenate([turned_high, turned_low], axis=1)
    products = dot(turned, pairs_ref[...])
    own = (iota((TAPROWS, 896), 0) >> 2) == (iota((TAPROWS, 896), 1) >> 5)
    folded = jnp.sum(jnp.where(own, products, 0.0).reshape(TAPROWS // 8, 8, 896), axis=0)
    lifted = folded[:, 0:128]
    for at in range(128, 896, 128):
        lifted = lifted + folded[:, at : at + 128]
    lifted = lifted + pltpu.roll(lifted, 64, 1)
    lifted = lifted + pltpu.roll(lifted, 32, 1)
    lifted = lifted + pltpu.roll(lifted, 4, 0)
    lanes = iota((8, 128), 1)
    shared = jnp.zeros((8, 128), F32)
    for b in range(4):
        rows = moments[8 * b : 8 * b + 8]
        rows = rows if b == 0 else pltpu.roll(rows, 4 * b, 1)
        shared = jnp.where((lanes >= 108 + 4 * b) & (lanes < 112 + 4 * b), rows, shared)
    upper = iota((8, 128), 0) < 4
    for k in range(4):
        first = pltpu.roll(lifted, 124 - 8 * k, 1)
        second = pltpu.roll(lifted, 120 - 8 * k, 1)
        columns = jnp.where(upper, first, second)
        message = jnp.where(lanes < 108, moments[8 * k : 8 * k + 8], shared)
        message = jnp.where(lanes >= 124, columns, message).astype(send_ref.dtype)
        send_ref[k] = jnp.broadcast_to(message[None], send_ref.shape[1:])
    for item in out_copies:
        item.wait()


def finish_kernel(scale, inv, recv_ref, taps_ref, owned_ref, conv_out, mix_out, lift_out):
    flat = recv_ref[...].reshape(1024, 128)
    total = dot(ones_where(iota((8, 1024), 0) == (iota((8, 1024), 1) & 7)), flat)
    high, low = split(total)
    both = jnp.concatenate([high.astype(F32), low.astype(F32)], axis=0).astype(BF16)
    conv = dot(both, taps_ref[...], NT)
    conv_out[0] = (conv[:8] + conv[8:]) * scale
    mixed = dot(owned_ref[...], both, NT) * (scale * inv)
    for b in range(4):
        rows = mixed[8 * b : 8 * b + 8]
        mix_out[0, :, 8 * b : 8 * b + 8] = rows[:, :8] + rows[:, 8:]
    lift_out[:, 0:4] = total[0:4, 124:128] * scale
    lift_out[:, 4:8] = total[4:8, 124:128] * scale


VMEM = pl.BlockSpec(memory_space=pltpu.VMEM)
HBM = pl.BlockSpec(memory_space=pltpu.HBM)


def in_hbm(array):
    return pltpu.with_memory_space_constraint(array, pltpu.HBM)


LIMIT = pltpu.CompilerParams(vmem_limit_bytes=20 * 1024 * 1024)


def on_device(micro_fields, lift_w, conv_w, mix_w, phi, psi, cotangent):
    micro = micro_fields[0]
    rank = phi.shape[0]
    cells = micro.shape[1] * micro.shape[2] * micro.shape[3]
    gx, gy, reps = lax.axis_size("gx"), lax.axis_size("gy"), lax.axis_size("rep")
    total_cells = cells * gx * gy
    inv = 1.0 / math.sqrt(total_cells) / math.sqrt(rank)
    scale = 1.0 / math.sqrt(total_cells * reps)
    codes = jnp.asarray(stack_codes())

    even = lax.axis_index("gx") % 2 == 0
    first, last = micro[:, 0], micro[:, -1]
    on_chip = [(i, i ^ 1) for i in range(gx)]
    off_chip = [(i, ((i + 1) ^ 1) - 1) for i in range(1, gx - 1)]
    near = lax.ppermute(jnp.where(even, last, first), "gx", on_chip)
    far = lax.ppermute(jnp.where(even, first, last), "gx", off_chip)

    rows = (rank // 4, 3 * rank // 8, 3 * rank // 8)
    parts, *pieces = pl.pallas_call(
        functools.partial(project_kernel, rows),
        in_specs=[HBM] * 3,
        out_specs=[HBM] + [VMEM] * EARLY,
        out_shape=[jax.ShapeDtypeStruct((gx * gy, 32, 128), BF16)]
        + [jax.ShapeDtypeStruct((rank // PIECES,) + psi.shape[1:], BF16)] * EARLY,
        scratch_shapes=[
            pltpu.VMEM(micro.shape, BF16),
            pltpu.VMEM(phi.shape, BF16),
            pltpu.VMEM((4, 32, 128), F32),
            pltpu.VMEM((gx * gy, 32, 128), BF16),
            pltpu.SemaphoreType.DMA((len(rows) + 2 + EARLY,)),
        ],
        compiler_params=pltpu.CompilerParams(vmem_limit_bytes=16 * 1024 * 1024),
        name="project",
    )(in_hbm(micro), in_hbm(phi), in_hbm(psi))

    gathered = lax.all_to_all(parts, ("gx", "gy"), 0, 0)

    weights, pairs, taps, owned = pl.pallas_call(
        functools.partial(stage_kernel, inv),
        in_specs=[VMEM] * 3,
        out_specs=[VMEM] * 4,
        out_shape=[
            jax.ShapeDtypeStruct((32, TAPROWS), BF16),
            jax.ShapeDtypeStruct((64, 896), BF16),
            jax.ShapeDtypeStruct((864, 128), BF16),
            jax.ShapeDtypeStruct((32, 128), BF16),
        ],
        compiler_params=pltpu.CompilerParams(vmem_limit_bytes=8 * 1024 * 1024),
        cost_estimate=pl.CostEstimate(flops=2_000_000_000, bytes_accessed=4_000_000, transcendentals=0),
        name="stage",
    )(lift_w, conv_w, mix_w)

    out_shape = jax.ShapeDtypeStruct((1, 32, 4, 16, 128), F32)
    out_field, send = pl.pallas_call(
        main_kernel,
        in_specs=[VMEM] * (7 + EARLY) + [HBM] * 2,
        out_specs=[HBM, VMEM],
        out_shape=[out_shape, jax.ShapeDtypeStruct((reps, gx * gy, 8, 128), BF16)],
        scratch_shapes=[
            pltpu.VMEM((512, STACK), BF16),
            pltpu.VMEM((STACK, 512), BF16),
            pltpu.VMEM((128, 4096), BF16),
            pltpu.VMEM((512, 512), F32),
            pltpu.VMEM((512, 512), BF16),
            pltpu.VMEM((512, STACK), F32),
            pltpu.VMEM((rank // PIECES * (PIECES - EARLY),) + psi.shape[1:], BF16),
            pltpu.VMEM(cotangent.shape, BF16),
            pltpu.VMEM(out_shape.shape, F32),
            pltpu.SemaphoreType.DMA((PIECES - EARLY + 3,)),
        ],
        compiler_params=LIMIT,
        cost_estimate=pl.CostEstimate(flops=4_000_000_000, bytes_accessed=6_000_000, transcendentals=500_000),
        name="layer",
    )(gathered, micro, near, far, weights, pairs, codes, *pieces, in_hbm(psi), in_hbm(cotangent))

    received = lax.all_to_all(send.reshape(reps * gx * gy, 8, 128), ("rep", "gx", "gy"), 0, 0)

    grads = pl.pallas_call(
        functools.partial(finish_kernel, scale, inv),
        in_specs=[VMEM] * 3,
        out_specs=[VMEM] * 3,
        out_shape=[
            jax.ShapeDtypeStruct((1, 8, 864), F32),
            jax.ShapeDtypeStruct((1, 8, 32), F32),
            jax.ShapeDtypeStruct((4, 8), F32),
        ],
        compiler_params=LIMIT,
        name="finish",
    )(received, taps, owned)
    return (out_field, *grads)


def solution(mesh):
    return jax.shard_map(
        on_device,
        mesh=mesh,
        in_specs=(
            P("rep", None, "gx", "gy", None),
            P(),
            P(),
            P(),
            P(None, "gx", "gy", None),
            P(None, "gx", "gy", None),
            P("rep", None, "gx", "gy", None),
        ),
        out_specs=(
            P("rep", None, "gx", "gy", None),
            P(None, "rep", None),
            P(None, "rep", None),
            P(None, "rep"),
        ),
        check_vma=False,
    )
```

```python
import functools
import math

import jax
import jax.numpy as jnp
import numpy as np
from jax import lax
from jax.experimental import pallas as pl
from jax.experimental.pallas import tpu as pltpu
from jax.sharding import PartitionSpec as P

F32 = jnp.float32
BF16 = jnp.bfloat16
NN = (((1,), (0,)), ((), ()))
NT = (((1,), (1,)), ((), ()))
TN = (((0,), (0,)), ((), ()))

STACK = 768
HALO_AT = 576
U_AT = 704
PIECES = 8
EARLY = 5
TAPROWS = 128


ROLLED = HALO_AT


def stack_codes():
    codes = np.full((8, STACK), -1, np.int32)
    codes[3] = -100
    for lane in range(STACK):
        if lane < HALO_AT:
            group, row = divmod(lane, 16)
            dx, dz, j = group // 12, group // 4 % 3, group % 4
        elif lane < HALO_AT + 72:
            at = lane - HALO_AT
            dx, dz, side, j = at // 24, at // 8 % 3, at // 4 % 2, at % 4
            row = 16 if side else -1
        elif lane >= U_AT:
            j, row = divmod(lane - U_AT, 16)
            codes[1, lane] = codes[4, lane] = 108 + j
            codes[3, lane], codes[5, lane] = row, 0
            continue
        else:
            continue
        for dy in range(3):
            codes[dy, lane] = (9 * dx + 3 * dy + dz) * 4 + j
        codes[3, lane], codes[5, lane] = row, 1
        if lane >= HALO_AT:
            codes[4, lane] = codes[2 if side else 0, lane]
        elif 7 <= row < 10:
            codes[4, lane] = codes[row - 7, lane]
    return codes


def dot(a, b, dims=NN):
    return lax.dot_general(a, b, dims, preferred_element_type=F32)


def split(values):
    high = values.astype(BF16)
    return high, (values - high.astype(F32)).astype(BF16)


def dot_split(a, b, dims=NN):
    high, low = split(a)
    return dot(high, b, dims) + dot(low, b, dims)


def iota(shape, dim):
    return lax.broadcasted_iota(jnp.int32, shape, dim)


def ones_where(condition):
    return jnp.where(condition, 1.0, 0.0).astype(BF16)


def row_sums(tiles):
    rows = iota((8, 128), 0)
    for step in (1, 2, 4):
        first = (rows & step) == 0
        tiles = [
            jnp.where(first, a, b) + pltpu.roll(jnp.where(first, b, a), 8 - step, 0)
            for a, b in zip(tiles[0::2], tiles[1::2])
        ]
    return tiles[0]


def selector(codes, dy):
    return ones_where(iota((TAPROWS, STACK), 0) == codes[dy : dy + 1, :])


def band(codes, dy):
    return (codes[3:4, :] - iota((16, STACK), 0)) == dy - 1


def lift_columns(lift, first):
    rows = iota((4, 128), 0)
    lanes = iota((4, 128), 1)
    if first is None:
        pick = ((lanes & 3) == rows) & (lanes < 108)
    else:
        pick = (lanes - first) == rows
    return dot(lift, ones_where(pick), TN)


def lift_blocks(lift):
    columns = lift_columns(lift, None)
    own = iota((27, 1, 128), 0) == (iota((27, 1, 128), 2) >> 2)
    return jnp.where(own, columns[None], 0.0).reshape(864, 128).astype(BF16)


def weight_table(weights, codes, table):
    spread = dot(weights, selector(codes, 4))
    valid = jnp.abs(codes[3:4, :] - iota((16, STACK), 0)) <= codes[5:6, :]
    for o in range(32):
        for at in range(0, STACK, 128):
            lanes = slice(at, at + 128)
            whole = jnp.broadcast_to(spread[o : o + 1, lanes], (16, 128))
            if at < ROLLED:
                rolled = pltpu.roll(whole, 120, 1, stride=1, stride_axis=0)
                if at + 128 > ROLLED:
                    rolled = jnp.where(iota((16, 128), 1) < ROLLED - at, rolled, whole)
                whole = rolled
            table[16 * o : 16 * o + 16, lanes] = jnp.where(valid[:, lanes], whole, 0.0).astype(BF16)


def stage_kernel(inv, lift_ref, conv_ref, mix_ref, weights_ref, pairs_ref, taps_ref, owned_ref):
    lift, conv, mix = lift_ref[...], conv_ref[0], mix_ref[0]
    blocks = lift_blocks(lift)
    taps_ref[...] = blocks
    own_lift = lift_columns(lift, 108)
    mixed = dot(mix, own_lift.astype(BF16), TN) * inv
    weights_ref[...] = (dot(conv, blocks) + mixed).astype(BF16)
    eye = ones_where(iota((32, 32), 0) == iota((32, 32), 1))
    turned = (dot(eye, mix, NT) * inv).astype(BF16)
    pairs = jnp.concatenate([conv, turned], axis=1)
    pairs_ref[...] = jnp.concatenate([pairs, pairs], axis=0)
    rep = lax.axis_index("rep")
    pick = ones_where(iota((8, 32), 1) == iota((8, 32), 0) + 8 * rep)
    mine = dot(pick, own_lift.astype(BF16))
    owned_ref[...] = jnp.concatenate(
        [mine if b == 0 else pltpu.roll(mine, 4 * b, 1) for b in range(4)], axis=0
    ).astype(BF16)


def project_kernel(parts, micro_ref, phi_ref, psi_ref, out_ref, *rest):
    pieces, (fields_ref, basis_ref, sums, message, sems) = rest[:EARLY], rest[EARLY:]

    def copy(at, count, sem):
        rows = pl.ds(at, count)
        return pltpu.make_async_copy(phi_ref.at[rows], basis_ref.at[rows], sem)

    starts = [sum(parts[:k]) for k in range(len(parts))]
    copies = [copy(at, count, sems.at[k]) for k, (at, count) in enumerate(zip(starts, parts))]
    own = pltpu.make_async_copy(micro_ref, fields_ref, sems.at[len(parts)])
    own.start()
    for item in copies:
        item.start()
    count = psi_ref.shape[0] // PIECES
    others = [
        pltpu.make_async_copy(
            psi_ref.at[pl.ds(k * count, count)], piece, sems.at[len(parts) + 2 + k]
        )
        for k, piece in enumerate(pieces)
    ]
    own.wait()
    fields = jnp.concatenate([fields_ref[:, x].reshape(64, 128) for x in range(4)], axis=1)
    me = lax.axis_index("gy")
    upper = iota((8, 128), 0) < 4
    edges = []
    for row in (0, 15):
        pick = ones_where(iota((8, 64), 1) == (iota((8, 64), 0) & 3) * 16 + row)
        edge = dot(pick, fields)
        halves = [
            jnp.where(upper, edge[:, at : at + 128], edge[:, at + 128 : at + 256]) for at in (0, 256)
        ]
        edges.append(jnp.concatenate(halves, axis=0))
    rims = [jnp.where(target > me, edges[1], edges[0]) for target in range(4)]
    for item, at, count in zip(copies, starts, parts):
        item.wait()
        if at == starts[1]:
            for other in others:
                other.start()
        wide = count * 16
        basis = jnp.concatenate(
            [basis_ref[at : at + count, x].reshape(wide, 128) for x in range(4)], axis=1
        )
        product = dot(fields, basis, NT)
        same = iota((16, 128), 0) == (iota((16, 128), 1) & 15)
        for chunk in range(0, count // 8, 4):
            row = at // 8 + chunk
            for pair in (0, 2):
                tiles = []
                for j in (pair, pair + 1):
                    for one in range(chunk, chunk + 4):
                        block = product[16 * j : 16 * j + 16, 128 * one : 128 * one + 128]
                        block = jnp.where(same, block, 0.0)
                        tiles.append(block[:8] + block[8:])
                packed = row_sums(tiles)
                sums[pair, row : row + 4, :] = packed[:4]
                sums[pair + 1, row : row + 4, :] = packed[4:]
    groups = ones_where(iota((8, 128), 0) == (iota((8, 128), 1) >> 4))
    first_part, rest = split(sums[...].reshape(128, 128))
    total = dot(groups, first_part, NT) + dot(groups, rest, NT)
    high = total.astype(BF16).astype(F32)
    for target in range(4):
        whole = jnp.concatenate([high, total - high, rims[target]], axis=0).astype(BF16)
        for plane in range(message.shape[0] // 4):
            message[4 * plane + target] = whole
    send = pltpu.make_async_copy(message, out_ref, sems.at[len(parts) + 1])
    send.start()
    for other in others:
        other.wait()
    send.wait()


def shift_z(values, dz):
    if dz == 0:
        return values
    lanes = iota(values.shape, 1) & 127
    width = values.shape[1]
    pieces = [
        pltpu.roll(values[:, at : at + 128], (-dz) % 128, 1) for at in range(0, width, 128)
    ]
    rolled = jnp.concatenate(pieces, axis=1)
    return jnp.where(lanes == (127 if dz > 0 else 0), 0.0, rolled)


def received_rims(parts_ref):
    gx, gy = lax.axis_index("gx"), lax.axis_index("gy")
    planes = parts_ref.shape[0] // 4

    def tile(plane, row, at):
        valid = (plane >= 0) & (plane < planes) & (row >= 0) & (row < 4)
        peer = jnp.clip(plane, 0, planes - 1) * 4 + jnp.clip(row, 0, 3)
        both = parts_ref[peer, 16:32, :].astype(F32)
        return jnp.where(valid, both[at : at + 8], 0.0)

    pieces = []
    lower = iota((8, 128), 0) < 4
    for x in range(6):
        plane = gx - 1 if x == 0 else gx + 1 if x == 5 else gx
        own = (x - 1) % 4
        below, above = [tile(plane, gy + step, 8 * (own // 2)) for step in (-1, 1)]
        if own % 2:
            below = pltpu.roll(below, 4, 0)
        else:
            above = pltpu.roll(above, 4, 0)
        pieces.append(jnp.where(lower, below, above))
    return jnp.concatenate(pieces, axis=1)


def main_kernel(parts_ref, micro_ref, near_ref, far_ref, weights_ref, pairs_ref, codes_ref, *rest):
    psi_refs = list(rest[:EARLY])
    psi_ref, cot_ref, out_ref, send_ref = rest[EARLY : EARLY + 4]
    table, stack, spread, pre, grad, corr, late_ref, cot, out, sems = rest[EARLY + 4 :]
    count = psi_ref.shape[0] // PIECES
    late = PIECES - EARLY
    copies = []
    for k in range(late):
        piece = late_ref.at[pl.ds(k * count, count)]
        copies.append(
            pltpu.make_async_copy(psi_ref.at[pl.ds((EARLY + k) * count, count)], piece, sems.at[k])
        )
        psi_refs.append(piece)
    cot_copy = pltpu.make_async_copy(cot_ref, cot, sems.at[late])
    for item in copies:
        item.start()
    codes = codes_ref[...]
    weight_table(weights_ref[...], codes, table)
    even = lax.axis_index("gx") % 2 == 0
    near, far = near_ref[...], far_ref[...]
    ends = jnp.where(even, far, near), jnp.where(even, near, far)
    planes = [ends[0]] + [micro_ref[:, x] for x in range(4)] + [ends[1]]
    fields = jnp.concatenate([plane.reshape(64, 128) for plane in planes], axis=1).astype(F32)
    rims = received_rims(parts_ref)
    rim_rows = {}
    for dz in range(3):
        moved = shift_z(fields, dz - 1).astype(BF16)
        moved_rim = shift_z(rims, dz - 1)
        for dx in range(3):
            at = (dx * 3 + dz) * 64
            stack[at : at + 64, :] = moved[:, 128 * dx : 128 * dx + 512]
            rim_rows[dx, dz] = moved_rim[:, 128 * dx : 128 * dx + 512]
    rim_block = jnp.concatenate([rim_rows[dx, dz] for dx in range(3) for dz in range(3)], axis=0)
    stack[HALO_AT:U_AT, :] = jnp.concatenate(
        [rim_block, jnp.zeros((U_AT - HALO_AT - 72, 512), F32)], axis=0
    ).astype(BF16)
    cot_copy.start()
    both = jnp.sum(parts_ref[:, 0:16, :].astype(F32), axis=0)
    high, low = split(both[:8] + both[8:])
    groups = ones_where(iota((8, 128), 0) == (iota((8, 128), 1) >> 4))
    same = ones_where(iota((16, 128), 0) == (iota((16, 128), 1) & 15))
    for part, values in enumerate((high, low)):
        expanded = dot(values, groups, TN)
        for j in range(4):
            for chunk in range(32):
                row = expanded[32 * j + chunk : 32 * j + chunk + 1, :]
                at = 64 * part + 16 * j
                spread[at : at + 16, 128 * chunk : 128 * chunk + 128] = (
                    jnp.broadcast_to(row, (16, 128)).astype(BF16) * same
                )
    fields = [jnp.zeros((128, 256), F32) for _ in range(2)]
    for k, piece in enumerate(psi_refs):
        if k == EARLY:
            for item in copies:
                item.wait()
        for pair in range(2):
            for row in range(0, count, 16):
                at = k * count + row
                basis = jnp.concatenate(
                    [piece[row : row + 16, 2 * pair + n].reshape(256, 128) for n in range(2)], axis=1
                )
                fields[pair] = fields[pair] + dot(spread[:, 16 * at : 16 * at + 256], basis)
    for pair, field in enumerate(fields):
        stack[U_AT:STACK, 256 * pair : 256 * pair + 256] = (field[:64] + field[64:]).astype(BF16)
    cot_copy.wait()
    out_copies = []
    for pair in range(2):
        half = slice(256 * pair, 256 * pair + 256)
        pre[:, half] = dot(table[...], stack[:, half])
        for o in range(32):
            rows = slice(16 * o, 16 * o + 16)
            for x in (2 * pair, 2 * pair + 1):
                lanes = slice(128 * x, 128 * x + 128)
                values = pre[rows, lanes]
                cumulative = 0.5 * (1.0 + lax.erf(values * (1.0 / math.sqrt(2.0))))
                density = jnp.exp(-0.5 * values * values) * (1.0 / math.sqrt(2.0 * math.pi))
                out[0, o, x] = values * cumulative
                slope = cumulative + values * density
                grad[rows, lanes] = (cot[0, o, x].astype(F32) * slope).astype(BF16)
        out_copies.append(
            pltpu.make_async_copy(
                out.at[:, :, pl.ds(2 * pair, 2)], out_ref.at[:, :, pl.ds(2 * pair, 2)], sems.at[late + 1 + pair]
            )
        )
        out_copies[-1].start()
        product = dot(grad[:, half], stack[:, half], NT)
        if pair == 0:
            corr[...] = product
        else:
            corr[...] += product
    bands = []
    for dy in range(3):
        valid = band(codes, dy)
        reduced = []
        for first in range(0, 32, 8):
            pieces = []
            for at in range(0, STACK, 128):
                lanes = slice(at, at + 128)
                tiles = []
                for o in range(first, first + 8):
                    block = jnp.where(valid[:, lanes], corr[16 * o : 16 * o + 16, lanes], 0.0)
                    tiles.append(block[:8] + block[8:])
                pieces.append(row_sums(tiles))
            reduced.append(jnp.concatenate(pieces, axis=1))
        bands.append(jnp.concatenate(reduced, axis=0))
    banded = jnp.concatenate(bands, axis=1)
    picks = jnp.concatenate([selector(codes, dy) for dy in range(3)], axis=1)
    high, low = split(banded)
    both = dot(jnp.concatenate([high, low], axis=0), picks, NT)
    moments = both[:32] + both[32:]
    turned_high, turned_low = split(moments.T)
    turned = jnp.concatenate([turned_high, turned_low], axis=1)
    products = dot(turned, pairs_ref[...])
    own = (iota((TAPROWS, 896), 0) >> 2) == (iota((TAPROWS, 896), 1) >> 5)
    folded = jnp.sum(jnp.where(own, products, 0.0).reshape(TAPROWS // 8, 8, 896), axis=0)
    lifted = folded[:, 0:128]
    for at in range(128, 896, 128):
        lifted = lifted + folded[:, at : at + 128]
    lifted = lifted + pltpu.roll(lifted, 64, 1)
    lifted = lifted + pltpu.roll(lifted, 32, 1)
    lifted = lifted + pltpu.roll(lifted, 4, 0)
    lanes = iota((8, 128), 1)
    shared = jnp.zeros((8, 128), F32)
    for b in range(4):
        rows = moments[8 * b : 8 * b + 8]
        rows = rows if b == 0 else pltpu.roll(rows, 4 * b, 1)
        shared = jnp.where((lanes >= 108 + 4 * b) & (lanes < 112 + 4 * b), rows, shared)
    upper = iota((8, 128), 0) < 4
    for k in range(4):
        first = pltpu.roll(lifted, 124 - 8 * k, 1)
        second = pltpu.roll(lifted, 120 - 8 * k, 1)
        columns = jnp.where(upper, first, second)
        message = jnp.where(lanes < 108, moments[8 * k : 8 * k + 8], shared)
        message = jnp.where(lanes >= 124, columns, message).astype(send_ref.dtype)
        send_ref[k] = jnp.broadcast_to(message[None], send_ref.shape[1:])
    for item in out_copies:
        item.wait()


def finish_kernel(scale, inv, recv_ref, taps_ref, owned_ref, conv_out, mix_out, lift_out):
    flat = recv_ref[...].reshape(1024, 128)
    total = dot(ones_where(iota((8, 1024), 0) == (iota((8, 1024), 1) & 7)), flat)
    high, low = split(total)
    both = jnp.concatenate([high.astype(F32), low.astype(F32)], axis=0).astype(BF16)
    conv = dot(both, taps_ref[...], NT)
    conv_out[0] = (conv[:8] + conv[8:]) * scale
    mixed = dot(owned_ref[...], both, NT) * (scale * inv)
    for b in range(4):
        rows = mixed[8 * b : 8 * b + 8]
        mix_out[0, :, 8 * b : 8 * b + 8] = rows[:, :8] + rows[:, 8:]
    lift_out[:, 0:4] = total[0:4, 124:128] * scale
    lift_out[:, 4:8] = total[4:8, 124:128] * scale


VMEM = pl.BlockSpec(memory_space=pltpu.VMEM)
HBM = pl.BlockSpec(memory_space=pltpu.HBM)


def in_hbm(array):
    return pltpu.with_memory_space_constraint(array, pltpu.HBM)


LIMIT = pltpu.CompilerParams(vmem_limit_bytes=20 * 1024 * 1024)


def on_device(micro_fields, lift_w, conv_w, mix_w, phi, psi, cotangent):
    micro = micro_fields[0]
    rank = phi.shape[0]
    cells = micro.shape[1] * micro.shape[2] * micro.shape[3]
    gx, gy, reps = lax.axis_size("gx"), lax.axis_size("gy"), lax.axis_size("rep")
    total_cells = cells * gx * gy
    inv = 1.0 / math.sqrt(total_cells) / math.sqrt(rank)
    scale = 1.0 / math.sqrt(total_cells * reps)
    codes = jnp.asarray(stack_codes())

    even = lax.axis_index("gx") % 2 == 0
    first, last = micro[:, 0], micro[:, -1]
    on_chip = [(i, i ^ 1) for i in range(gx)]
    off_chip = [(i, ((i + 1) ^ 1) - 1) for i in range(1, gx - 1)]
    near = lax.ppermute(jnp.where(even, last, first), "gx", on_chip)
    far = lax.ppermute(jnp.where(even, first, last), "gx", off_chip)

    rows = (rank // 4,) * 4
    parts, *pieces = pl.pallas_call(
        functools.partial(project_kernel, rows),
        in_specs=[HBM] * 3,
        out_specs=[HBM] + [VMEM] * EARLY,
        out_shape=[jax.ShapeDtypeStruct((gx * gy, 32, 128), BF16)]
        + [jax.ShapeDtypeStruct((rank // PIECES,) + psi.shape[1:], BF16)] * EARLY,
        scratch_shapes=[
            pltpu.VMEM(micro.shape, BF16),
            pltpu.VMEM(phi.shape, BF16),
            pltpu.VMEM((4, 32, 128), F32),
            pltpu.VMEM((gx * gy, 32, 128), BF16),
            pltpu.SemaphoreType.DMA((len(rows) + 2 + EARLY,)),
        ],
        compiler_params=pltpu.CompilerParams(vmem_limit_bytes=16 * 1024 * 1024),
        name="project",
    )(in_hbm(micro), in_hbm(phi), in_hbm(psi))

    gathered = lax.all_to_all(parts, ("gx", "gy"), 0, 0)

    weights, pairs, taps, owned = pl.pallas_call(
        functools.partial(stage_kernel, inv),
        in_specs=[VMEM] * 3,
        out_specs=[VMEM] * 4,
        out_shape=[
            jax.ShapeDtypeStruct((32, TAPROWS), BF16),
            jax.ShapeDtypeStruct((64, 896), BF16),
            jax.ShapeDtypeStruct((864, 128), BF16),
            jax.ShapeDtypeStruct((32, 128), BF16),
        ],
        compiler_params=pltpu.CompilerParams(vmem_limit_bytes=8 * 1024 * 1024),
        cost_estimate=pl.CostEstimate(flops=2_000_000_000, bytes_accessed=4_000_000, transcendentals=0),
        name="stage",
    )(lift_w, conv_w, mix_w)

    out_shape = jax.ShapeDtypeStruct((1, 32, 4, 16, 128), F32)
    out_field, send = pl.pallas_call(
        main_kernel,
        in_specs=[VMEM] * (7 + EARLY) + [HBM] * 2,
        out_specs=[HBM, VMEM],
        out_shape=[out_shape, jax.ShapeDtypeStruct((reps, gx * gy, 8, 128), BF16)],
        scratch_shapes=[
            pltpu.VMEM((512, STACK), BF16),
            pltpu.VMEM((STACK, 512), BF16),
            pltpu.VMEM((128, 4096), BF16),
            pltpu.VMEM((512, 512), F32),
            pltpu.VMEM((512, 512), BF16),
            pltpu.VMEM((512, STACK), F32),
            pltpu.VMEM((rank // PIECES * (PIECES - EARLY),) + psi.shape[1:], BF16),
            pltpu.VMEM(cotangent.shape, BF16),
            pltpu.VMEM(out_shape.shape, F32),
            pltpu.SemaphoreType.DMA((PIECES - EARLY + 3,)),
        ],
        compiler_params=LIMIT,
        cost_estimate=pl.CostEstimate(flops=4_000_000_000, bytes_accessed=6_000_000, transcendentals=500_000),
        name="layer",
    )(gathered, micro, near, far, weights, pairs, codes, *pieces, in_hbm(psi), in_hbm(cotangent))

    received = lax.all_to_all(send.reshape(reps * gx * gy, 8, 128), ("rep", "gx", "gy"), 0, 0)

    grads = pl.pallas_call(
        functools.partial(finish_kernel, scale, inv),
        in_specs=[VMEM] * 3,
        out_specs=[VMEM] * 3,
        out_shape=[
            jax.ShapeDtypeStruct((1, 8, 864), F32),
            jax.ShapeDtypeStruct((1, 8, 32), F32),
            jax.ShapeDtypeStruct((4, 8), F32),
        ],
        compiler_params=LIMIT,
        name="finish",
    )(received, taps, owned)
    return (out_field, *grads)


def solution(mesh):
    return jax.shard_map(
        on_device,
        mesh=mesh,
        in_specs=(
            P("rep", None, "gx", "gy", None),
            P(),
            P(),
            P(),
            P(None, "gx", "gy", None),
            P(None, "gx", "gy", None),
            P("rep", None, "gx", "gy", None),
        ),
        out_specs=(
            P("rep", None, "gx", "gy", None),
            P(None, "rep", None),
            P(None, "rep", None),
            P(None, "rep"),
        ),
        check_vma=False,
    )
```

```python
import functools
import math

import jax
import jax.numpy as jnp
import numpy as np
from jax import lax
from jax.experimental import pallas as pl
from jax.experimental.pallas import tpu as pltpu
from jax.sharding import PartitionSpec as P

F32 = jnp.float32
BF16 = jnp.bfloat16
NN = (((1,), (0,)), ((), ()))
NT = (((1,), (1,)), ((), ()))
TN = (((0,), (0,)), ((), ()))

STACK = 768
HALO_AT = 576
U_AT = 704
PIECES = 8
EARLY = 5
TAPROWS = 128


ROLLED = HALO_AT


def stack_codes():
    codes = np.full((8, STACK), -1, np.int32)
    codes[3] = -100
    for lane in range(STACK):
        if lane < HALO_AT:
            group, row = divmod(lane, 16)
            dx, dz, j = group // 12, group // 4 % 3, group % 4
        elif lane < HALO_AT + 72:
            at = lane - HALO_AT
            dx, dz, side, j = at // 24, at // 8 % 3, at // 4 % 2, at % 4
            row = 16 if side else -1
        elif lane >= U_AT:
            j, row = divmod(lane - U_AT, 16)
            codes[1, lane] = codes[4, lane] = 108 + j
            codes[3, lane], codes[5, lane] = row, 0
            continue
        else:
            continue
        for dy in range(3):
            codes[dy, lane] = (9 * dx + 3 * dy + dz) * 4 + j
        codes[3, lane], codes[5, lane] = row, 1
        if lane >= HALO_AT:
            codes[4, lane] = codes[2 if side else 0, lane]
        elif 7 <= row < 10:
            codes[4, lane] = codes[row - 7, lane]
    return codes


def dot(a, b, dims=NN):
    return lax.dot_general(a, b, dims, preferred_element_type=F32)


def split(values):
    high = values.astype(BF16)
    return high, (values - high.astype(F32)).astype(BF16)


def dot_split(a, b, dims=NN):
    high, low = split(a)
    return dot(high, b, dims) + dot(low, b, dims)


def iota(shape, dim):
    return lax.broadcasted_iota(jnp.int32, shape, dim)


def ones_where(condition):
    return jnp.where(condition, 1.0, 0.0).astype(BF16)


def row_sums(tiles):
    rows = iota((8, 128), 0)
    for step in (1, 2, 4):
        first = (rows & step) == 0
        tiles = [
            jnp.where(first, a, b) + pltpu.roll(jnp.where(first, b, a), 8 - step, 0)
            for a, b in zip(tiles[0::2], tiles[1::2])
        ]
    return tiles[0]


def selector(codes, dy):
    return ones_where(iota((TAPROWS, STACK), 0) == codes[dy : dy + 1, :])


def band(codes, dy):
    return (codes[3:4, :] - iota((16, STACK), 0)) == dy - 1


def lift_columns(lift, first):
    rows = iota((4, 128), 0)
    lanes = iota((4, 128), 1)
    if first is None:
        pick = ((lanes & 3) == rows) & (lanes < 108)
    else:
        pick = (lanes - first) == rows
    return dot(lift, ones_where(pick), TN)


def lift_blocks(lift):
    columns = lift_columns(lift, None)
    own = iota((27, 1, 128), 0) == (iota((27, 1, 128), 2) >> 2)
    return jnp.where(own, columns[None], 0.0).reshape(864, 128).astype(BF16)


def weight_table(weights, codes, table):
    spread = dot(weights, selector(codes, 4))
    valid = jnp.abs(codes[3:4, :] - iota((16, STACK), 0)) <= codes[5:6, :]
    for o in range(32):
        for at in range(0, STACK, 128):
            lanes = slice(at, at + 128)
            whole = jnp.broadcast_to(spread[o : o + 1, lanes], (16, 128))
            if at < ROLLED:
                rolled = pltpu.roll(whole, 120, 1, stride=1, stride_axis=0)
                if at + 128 > ROLLED:
                    rolled = jnp.where(iota((16, 128), 1) < ROLLED - at, rolled, whole)
                whole = rolled
            table[16 * o : 16 * o + 16, lanes] = jnp.where(valid[:, lanes], whole, 0.0).astype(BF16)


def stage_kernel(inv, lift_ref, conv_ref, mix_ref, weights_ref, pairs_ref, taps_ref, owned_ref):
    lift, conv, mix = lift_ref[...], conv_ref[0], mix_ref[0]
    blocks = lift_blocks(lift)
    taps_ref[...] = blocks
    own_lift = lift_columns(lift, 108)
    mixed = dot(mix, own_lift.astype(BF16), TN) * inv
    weights_ref[...] = (dot(conv, blocks) + mixed).astype(BF16)
    eye = ones_where(iota((32, 32), 0) == iota((32, 32), 1))
    turned = (dot(eye, mix, NT) * inv).astype(BF16)
    pairs = jnp.concatenate([conv, turned], axis=1)
    pairs_ref[...] = jnp.concatenate([pairs, pairs], axis=0)
    rep = lax.axis_index("rep")
    pick = ones_where(iota((8, 32), 1) == iota((8, 32), 0) + 8 * rep)
    mine = dot(pick, own_lift.astype(BF16))
    owned_ref[...] = jnp.concatenate(
        [mine if b == 0 else pltpu.roll(mine, 4 * b, 1) for b in range(4)], axis=0
    ).astype(BF16)


def project_kernel(parts, micro_ref, phi_ref, psi_ref, out_ref, *rest):
    pieces, (fields_ref, basis_ref, sums, message, sems) = rest[:EARLY], rest[EARLY:]

    def copy(at, count, sem):
        rows = pl.ds(at, count)
        return pltpu.make_async_copy(phi_ref.at[rows], basis_ref.at[rows], sem)

    starts = [sum(parts[:k]) for k in range(len(parts))]
    copies = [copy(at, count, sems.at[k]) for k, (at, count) in enumerate(zip(starts, parts))]
    own = pltpu.make_async_copy(micro_ref, fields_ref, sems.at[len(parts)])
    own.start()
    for item in copies:
        item.start()
    count = psi_ref.shape[0] // PIECES
    others = [
        pltpu.make_async_copy(
            psi_ref.at[pl.ds(k * count, count)], piece, sems.at[len(parts) + 2 + k]
        )
        for k, piece in enumerate(pieces)
    ]
    own.wait()
    fields = jnp.concatenate([fields_ref[:, x].reshape(64, 128) for x in range(4)], axis=1)
    me = lax.axis_index("gy")
    upper = iota((8, 128), 0) < 4
    edges = []
    for row in (0, 15):
        pick = ones_where(iota((8, 64), 1) == (iota((8, 64), 0) & 3) * 16 + row)
        edge = dot(pick, fields)
        halves = [
            jnp.where(upper, edge[:, at : at + 128], edge[:, at + 128 : at + 256]) for at in (0, 256)
        ]
        edges.append(jnp.concatenate(halves, axis=0))
    rims = [jnp.where(target > me, edges[1], edges[0]) for target in range(4)]
    for item, at, count in zip(copies, starts, parts):
        item.wait()
        if at == starts[1]:
            for other in others:
                other.start()
        wide = count * 16
        basis = jnp.concatenate(
            [basis_ref[at : at + count, x].reshape(wide, 128) for x in range(4)], axis=1
        )
        product = dot(fields, basis, NT)
        same = iota((16, 128), 0) == (iota((16, 128), 1) & 15)
        for chunk in range(0, count // 8, 4):
            row = at // 8 + chunk
            for pair in (0, 2):
                tiles = []
                for j in (pair, pair + 1):
                    for one in range(chunk, chunk + 4):
                        block = product[16 * j : 16 * j + 16, 128 * one : 128 * one + 128]
                        block = jnp.where(same, block, 0.0)
                        tiles.append(block[:8] + block[8:])
                packed = row_sums(tiles)
                sums[pair, row : row + 4, :] = packed[:4]
                sums[pair + 1, row : row + 4, :] = packed[4:]
    groups = ones_where(iota((8, 128), 0) == (iota((8, 128), 1) >> 4))
    first_part, rest = split(sums[...].reshape(128, 128))
    total = dot(groups, first_part, NT) + dot(groups, rest, NT)
    high = total.astype(BF16).astype(F32)
    for target in range(4):
        whole = jnp.concatenate([high, total - high, rims[target]], axis=0).astype(BF16)
        for plane in range(message.shape[0] // 4):
            message[4 * plane + target] = whole
    send = pltpu.make_async_copy(message, out_ref, sems.at[len(parts) + 1])
    send.start()
    for other in others:
        other.wait()
    send.wait()


def shift_z(values, dz):
    if dz == 0:
        return values
    lanes = iota(values.shape, 1) & 127
    width = values.shape[1]
    pieces = [
        pltpu.roll(values[:, at : at + 128], (-dz) % 128, 1) for at in range(0, width, 128)
    ]
    rolled = jnp.concatenate(pieces, axis=1)
    return jnp.where(lanes == (127 if dz > 0 else 0), 0.0, rolled)


def received_rims(parts_ref):
    gx, gy = lax.axis_index("gx"), lax.axis_index("gy")
    planes = parts_ref.shape[0] // 4

    def tile(plane, row, at):
        valid = (plane >= 0) & (plane < planes) & (row >= 0) & (row < 4)
        peer = jnp.clip(plane, 0, planes - 1) * 4 + jnp.clip(row, 0, 3)
        both = parts_ref[peer, 16:32, :].astype(F32)
        return jnp.where(valid, both[at : at + 8], 0.0)

    pieces = []
    lower = iota((8, 128), 0) < 4
    for x in range(6):
        plane = gx - 1 if x == 0 else gx + 1 if x == 5 else gx
        own = (x - 1) % 4
        below, above = [tile(plane, gy + step, 8 * (own // 2)) for step in (-1, 1)]
        if own % 2:
            below = pltpu.roll(below, 4, 0)
        else:
            above = pltpu.roll(above, 4, 0)
        pieces.append(jnp.where(lower, below, above))
    return jnp.concatenate(pieces, axis=1)


def main_kernel(parts_ref, micro_ref, near_ref, far_ref, weights_ref, pairs_ref, codes_ref, *rest):
    psi_refs = list(rest[:EARLY])
    psi_ref, cot_ref, out_ref, send_ref = rest[EARLY : EARLY + 4]
    table, stack, spread, pre, grad, corr, late_ref, cot, out, sems = rest[EARLY + 4 :]
    count = psi_ref.shape[0] // PIECES
    late = PIECES - EARLY
    copies = []
    for k in range(late):
        piece = late_ref.at[pl.ds(k * count, count)]
        copies.append(
            pltpu.make_async_copy(psi_ref.at[pl.ds((EARLY + k) * count, count)], piece, sems.at[k])
        )
        psi_refs.append(piece)
    cot_copy = pltpu.make_async_copy(cot_ref, cot, sems.at[late])
    for item in copies:
        item.start()
    codes = codes_ref[...]
    weight_table(weights_ref[...], codes, table)
    even = lax.axis_index("gx") % 2 == 0
    near, far = near_ref[...], far_ref[...]
    ends = jnp.where(even, far, near), jnp.where(even, near, far)
    planes = [ends[0]] + [micro_ref[:, x] for x in range(4)] + [ends[1]]
    fields = jnp.concatenate([plane.reshape(64, 128) for plane in planes], axis=1).astype(F32)
    rims = received_rims(parts_ref)
    rim_rows = {}
    for dz in range(3):
        moved = shift_z(fields, dz - 1).astype(BF16)
        moved_rim = shift_z(rims, dz - 1)
        for dx in range(3):
            at = (dx * 3 + dz) * 64
            stack[at : at + 64, :] = moved[:, 128 * dx : 128 * dx + 512]
            rim_rows[dx, dz] = moved_rim[:, 128 * dx : 128 * dx + 512]
    rim_block = jnp.concatenate([rim_rows[dx, dz] for dx in range(3) for dz in range(3)], axis=0)
    stack[HALO_AT:U_AT, :] = jnp.concatenate(
        [rim_block, jnp.zeros((U_AT - HALO_AT - 72, 512), F32)], axis=0
    ).astype(BF16)
    cot_copy.start()
    both = jnp.sum(parts_ref[:, 0:16, :].astype(F32), axis=0)
    high, low = split(both[:8] + both[8:])
    groups = ones_where(iota((8, 128), 0) == (iota((8, 128), 1) >> 4))
    same = iota((16, 128), 0) == (iota((16, 128), 1) & 15)
    for part, values in enumerate((high, low)):
        expanded = dot(values, groups, TN)
        for j in range(4):
            for chunk in range(32):
                row = expanded[32 * j + chunk : 32 * j + chunk + 1, :]
                at = 64 * part + 16 * j
                spread[at : at + 16, 128 * chunk : 128 * chunk + 128] = jnp.where(
                    same, row, 0.0
                ).astype(BF16)
    fields = [jnp.zeros((128, 256), F32) for _ in range(2)]
    for k, piece in enumerate(psi_refs):
        if k >= EARLY:
            copies[k - EARLY].wait()
        for pair in range(2):
            for row in range(0, count, 16):
                at = k * count + row
                basis = jnp.concatenate(
                    [piece[row : row + 16, 2 * pair + n].reshape(256, 128) for n in range(2)], axis=1
                )
                fields[pair] = fields[pair] + dot(spread[:, 16 * at : 16 * at + 256], basis)
    for pair, field in enumerate(fields):
        stack[U_AT:STACK, 256 * pair : 256 * pair + 256] = (field[:64] + field[64:]).astype(BF16)
    out_copies = []
    for pair in range(2):
        half = slice(256 * pair, 256 * pair + 256)
        pre[:, half] = dot(table[...], stack[:, half])
        if pair == 0:
            cot_copy.wait()
        for o in range(32):
            rows = slice(16 * o, 16 * o + 16)
            for x in (2 * pair, 2 * pair + 1):
                lanes = slice(128 * x, 128 * x + 128)
                values = pre[rows, lanes]
                cumulative = 0.5 * (1.0 + lax.erf(values * (1.0 / math.sqrt(2.0))))
                density = jnp.exp(-0.5 * values * values) * (1.0 / math.sqrt(2.0 * math.pi))
                out[0, o, x] = values * cumulative
                slope = cumulative + values * density
                grad[rows, lanes] = (cot[0, o, x].astype(F32) * slope).astype(BF16)
        out_copies.append(
            pltpu.make_async_copy(
                out.at[:, :, pl.ds(2 * pair, 2)], out_ref.at[:, :, pl.ds(2 * pair, 2)], sems.at[late + 1 + pair]
            )
        )
        out_copies[-1].start()
        product = dot(grad[:, half], stack[:, half], NT)
        if pair == 0:
            corr[...] = product
        else:
            corr[...] += product
    bands = []
    for dy in range(3):
        valid = band(codes, dy)
        reduced = []
        for first in range(0, 32, 8):
            pieces = []
            for at in range(0, STACK, 128):
                lanes = slice(at, at + 128)
                tiles = []
                for o in range(first, first + 8):
                    block = jnp.where(valid[:, lanes], corr[16 * o : 16 * o + 16, lanes], 0.0)
                    tiles.append(block[:8] + block[8:])
                pieces.append(row_sums(tiles))
            reduced.append(jnp.concatenate(pieces, axis=1))
        bands.append(jnp.concatenate(reduced, axis=0))
    banded = jnp.concatenate(bands, axis=1)
    picks = jnp.concatenate([selector(codes, dy) for dy in range(3)], axis=1)
    high, low = split(banded)
    both = dot(jnp.concatenate([high, low], axis=0), picks, NT)
    moments = both[:32] + both[32:]
    turned_high, turned_low = split(moments.T)
    turned = jnp.concatenate([turned_high, turned_low], axis=1)
    products = dot(turned, pairs_ref[...])
    own = (iota((TAPROWS, 896), 0) >> 2) == (iota((TAPROWS, 896), 1) >> 5)
    folded = jnp.sum(jnp.where(own, products, 0.0).reshape(TAPROWS // 8, 8, 896), axis=0)
    lifted = folded[:, 0:128]
    for at in range(128, 896, 128):
        lifted = lifted + folded[:, at : at + 128]
    lifted = lifted + pltpu.roll(lifted, 64, 1)
    lifted = lifted + pltpu.roll(lifted, 32, 1)
    lifted = lifted + pltpu.roll(lifted, 4, 0)
    lanes = iota((8, 128), 1)
    shared = jnp.zeros((8, 128), F32)
    for b in range(4):
        rows = moments[8 * b : 8 * b + 8]
        rows = rows if b == 0 else pltpu.roll(rows, 4 * b, 1)
        shared = jnp.where((lanes >= 108 + 4 * b) & (lanes < 112 + 4 * b), rows, shared)
    upper = iota((8, 128), 0) < 4
    for k in range(4):
        first = pltpu.roll(lifted, 124 - 8 * k, 1)
        second = pltpu.roll(lifted, 120 - 8 * k, 1)
        columns = jnp.where(upper, first, second)
        message = jnp.where(lanes < 108, moments[8 * k : 8 * k + 8], shared)
        message = jnp.where(lanes >= 124, columns, message).astype(send_ref.dtype)
        send_ref[k] = jnp.broadcast_to(message[None], send_ref.shape[1:])
    for item in out_copies:
        item.wait()


def finish_kernel(scale, inv, recv_ref, taps_ref, owned_ref, conv_out, mix_out, lift_out):
    flat = recv_ref[...].reshape(1024, 128)
    total = dot(ones_where(iota((8, 1024), 0) == (iota((8, 1024), 1) & 7)), flat)
    high, low = split(total)
    both = jnp.concatenate([high.astype(F32), low.astype(F32)], axis=0).astype(BF16)
    conv = dot(both, taps_ref[...], NT)
    conv_out[0] = (conv[:8] + conv[8:]) * scale
    mixed = dot(owned_ref[...], both, NT) * (scale * inv)
    for b in range(4):
        rows = mixed[8 * b : 8 * b + 8]
        mix_out[0, :, 8 * b : 8 * b + 8] = rows[:, :8] + rows[:, 8:]
    lift_out[:, 0:4] = total[0:4, 124:128] * scale
    lift_out[:, 4:8] = total[4:8, 124:128] * scale


VMEM = pl.BlockSpec(memory_space=pltpu.VMEM)
HBM = pl.BlockSpec(memory_space=pltpu.HBM)


def in_hbm(array):
    return pltpu.with_memory_space_constraint(array, pltpu.HBM)


LIMIT = pltpu.CompilerParams(vmem_limit_bytes=20 * 1024 * 1024)


def on_device(micro_fields, lift_w, conv_w, mix_w, phi, psi, cotangent):
    micro = micro_fields[0]
    rank = phi.shape[0]
    cells = micro.shape[1] * micro.shape[2] * micro.shape[3]
    gx, gy, reps = lax.axis_size("gx"), lax.axis_size("gy"), lax.axis_size("rep")
    total_cells = cells * gx * gy
    inv = 1.0 / math.sqrt(total_cells) / math.sqrt(rank)
    scale = 1.0 / math.sqrt(total_cells * reps)
    codes = jnp.asarray(stack_codes())

    even = lax.axis_index("gx") % 2 == 0
    first, last = micro[:, 0], micro[:, -1]
    on_chip = [(i, i ^ 1) for i in range(gx)]
    off_chip = [(i, ((i + 1) ^ 1) - 1) for i in range(1, gx - 1)]
    near = lax.ppermute(jnp.where(even, last, first), "gx", on_chip)
    far = lax.ppermute(jnp.where(even, first, last), "gx", off_chip)

    rows = (rank // 4, 3 * rank // 8, 3 * rank // 8)
    parts, *pieces = pl.pallas_call(
        functools.partial(project_kernel, rows),
        in_specs=[HBM] * 3,
        out_specs=[HBM] + [VMEM] * EARLY,
        out_shape=[jax.ShapeDtypeStruct((gx * gy, 32, 128), BF16)]
        + [jax.ShapeDtypeStruct((rank // PIECES,) + psi.shape[1:], BF16)] * EARLY,
        scratch_shapes=[
            pltpu.VMEM(micro.shape, BF16),
            pltpu.VMEM(phi.shape, BF16),
            pltpu.VMEM((4, 32, 128), F32),
            pltpu.VMEM((gx * gy, 32, 128), BF16),
            pltpu.SemaphoreType.DMA((len(rows) + 2 + EARLY,)),
        ],
        compiler_params=pltpu.CompilerParams(vmem_limit_bytes=16 * 1024 * 1024),
        name="project",
    )(in_hbm(micro), in_hbm(phi), in_hbm(psi))

    gathered = lax.all_to_all(parts, ("gx", "gy"), 0, 0)

    weights, pairs, taps, owned = pl.pallas_call(
        functools.partial(stage_kernel, inv),
        in_specs=[VMEM] * 3,
        out_specs=[VMEM] * 4,
        out_shape=[
            jax.ShapeDtypeStruct((32, TAPROWS), BF16),
            jax.ShapeDtypeStruct((64, 896), BF16),
            jax.ShapeDtypeStruct((864, 128), BF16),
            jax.ShapeDtypeStruct((32, 128), BF16),
        ],
        compiler_params=pltpu.CompilerParams(vmem_limit_bytes=8 * 1024 * 1024),
        cost_estimate=pl.CostEstimate(flops=2_000_000_000, bytes_accessed=4_000_000, transcendentals=0),
        name="stage",
    )(lift_w, conv_w, mix_w)

    out_shape = jax.ShapeDtypeStruct((1, 32, 4, 16, 128), F32)
    out_field, send = pl.pallas_call(
        main_kernel,
        in_specs=[VMEM] * (7 + EARLY) + [HBM] * 2,
        out_specs=[HBM, VMEM],
        out_shape=[out_shape, jax.ShapeDtypeStruct((reps, gx * gy, 8, 128), BF16)],
        scratch_shapes=[
            pltpu.VMEM((512, STACK), BF16),
            pltpu.VMEM((STACK, 512), BF16),
            pltpu.VMEM((128, 4096), BF16),
            pltpu.VMEM((512, 512), F32),
            pltpu.VMEM((512, 512), BF16),
            pltpu.VMEM((512, STACK), F32),
            pltpu.VMEM((rank // PIECES * (PIECES - EARLY),) + psi.shape[1:], BF16),
            pltpu.VMEM(cotangent.shape, BF16),
            pltpu.VMEM(out_shape.shape, F32),
            pltpu.SemaphoreType.DMA((PIECES - EARLY + 3,)),
        ],
        compiler_params=LIMIT,
        cost_estimate=pl.CostEstimate(flops=4_000_000_000, bytes_accessed=6_000_000, transcendentals=500_000),
        name="layer",
    )(gathered, micro, near, far, weights, pairs, codes, *pieces, in_hbm(psi), in_hbm(cotangent))

    received = lax.all_to_all(send.reshape(reps * gx * gy, 8, 128), ("rep", "gx", "gy"), 0, 0)

    grads = pl.pallas_call(
        functools.partial(finish_kernel, scale, inv),
        in_specs=[VMEM] * 3,
        out_specs=[VMEM] * 3,
        out_shape=[
            jax.ShapeDtypeStruct((1, 8, 864), F32),
            jax.ShapeDtypeStruct((1, 8, 32), F32),
            jax.ShapeDtypeStruct((4, 8), F32),
        ],
        compiler_params=LIMIT,
        name="finish",
    )(received, taps, owned)
    return (out_field, *grads)


def solution(mesh):
    return jax.shard_map(
        on_device,
        mesh=mesh,
        in_specs=(
            P("rep", None, "gx", "gy", None),
            P(),
            P(),
            P(),
            P(None, "gx", "gy", None),
            P(None, "gx", "gy", None),
            P("rep", None, "gx", "gy", None),
        ),
        out_specs=(
            P("rep", None, "gx", "gy", None),
            P(None, "rep", None),
            P(None, "rep", None),
            P(None, "rep"),
        ),
        check_vma=False,
    )
```
